32 devices in a mesh: parts: 1, prow: 32 (over z, y, x, core), pcol: 1.
Axes of the slice: x: 2, y: 2, z: 4, core: 2. Of those that a mesh axis runs over, the one named last changes fastest.
Arguments:
- rhs: bfloat16 [3, 32, 128, 128], P('parts', 'prow', 'pcol'), may hold values from -6 to 6
- lower_factor_t: bfloat16 [3, 32, 128, 3, 32, 128], P('parts', 'pcol', None, None, 'prow'), may hold values from -0.1875 to 0.1875
- upper_factor_t: bfloat16 [3, 32, 128, 3, 32, 128], P('parts', 'pcol', None, None, 'prow'), may hold values from -0.1875 to 0.1875
- lower_snode: int32 [64], P('parts'), may hold values from 0 to 4, never falling along the last dimension, each value on 1 to 16 neighbouring positions
- upper_snode: int32 [32], P('parts'), may hold values from 0 to 3, never falling along the last dimension, each value on 1 to 16 neighbouring positions
- parent: int32 [5, 1], P('parts'), may hold values from 0 to 3
- pattern: int32 [32, 5], P('parts'), may hold values 0 or 1
Outputs:
- forward_solution: float32 [3, 32, 128, 128], P('parts', 'prow', 'pcol')
- backward_solution: float32 [3, 32, 128, 128], P('parts', 'prow', 'pcol')
The draws below stay inside these ranges and needn't reach their ends.
Inputs may be any that keep to these rules, and one draw needn't show every extreme that they name: `lower_snode`: never falls; each supernode spans 1 to 16 blocks of 128 rows and every number from 0 to 4 is used. `upper_snode`: never falls; each supernode spans 1 to 16 blocks of 128 rows and every number from 0 to 3 is used. Every upper supernode is the parent of at least one lower supernode.
All inputs are finite; a program needn't handle non-finite values.
Results may differ from the reference program's by a relative error of at most 0.0042.
Values may be sent and summed in bfloat16 or wider, within the bound.
No kernel may reach another device: no remote copies, remote signals or barrier semaphores. Data moves between devices by JAX's collectives and lax.ppermute only.
A program may use at most 128 MiB of HBM per device.

```python
import math
import jax
import jax.numpy as jnp
import numpy as np
from jax import lax

BS = 128
RHS = 128
NBR = 3
LB = 64
UB = 32
NB = 96
LCOUNT = 5
UCOUNT = 4
N_PROW = 32


def set_ends(array, stream_key, least, top_value):
    shape = array.shape
    index_at = [jax.random.randint(jax.random.fold_in(stream_key, axis), (), 0, shape[axis]) for axis in range(len(shape))]
    array = array.at[tuple(index_at)].set(least)
    longest = shape.index(max(shape))
    index_at[longest] = (index_at[longest] + 1) % shape[longest]
    return array.at[tuple(index_at)].set(top_value)


def level_of(own_key, dims, cuts, least, largest):
    factor_of = 1.0
    for position, shards_of in cuts:
        heights = jax.random.uniform(jax.random.fold_in(jax.random.fold_in(own_key, 6), position), (shards_of,), jnp.float32, least / len(cuts), largest / len(cuts))
        factor_of = factor_of * jnp.repeat(jnp.exp(heights), dims[position] // shards_of).reshape((-1,) + (1,) * (len(dims) - 1 - position))
    return factor_of


def different_ones(rng, rows, number_of, top, lift):
    order = jax.random.permutation(jax.random.fold_in(rng, 1), number_of)
    boost = order
    for power in range(3):
        boost = boost * boost // number_of
    boost = boost * lift // number_of
    lots = jax.random.randint(jax.random.fold_in(rng, 2), (rows, number_of), 0, 4096) + boost
    fixed_rows = jax.random.permutation(jax.random.fold_in(rng, 3), rows)[jnp.arange(number_of) % rows]
    lots = jnp.where(jnp.arange(rows)[:, None] == fixed_rows[None, :], 1 << 14, lots)
    merit = lots * number_of + jnp.arange(number_of)
    return lax.top_k(merit.astype(jnp.int32), top)[1].astype(jnp.int32)


def length_profile(number_of, total, limit, slope):
    weights = [(1 << 20) // math.isqrt(grade ** slope) + 1 for grade in range(2, number_of + 1)]
    spare, holding = total - limit - (number_of - 1), [1] * (number_of - 1)
    while spare > 0:
        movable = [i for i in range(number_of - 1) if holding[i] < limit]
        pool, budget = sum([weights[i] for i in movable]), spare
        for i in movable:
            more = min(limit - holding[i], max(1, budget * weights[i] // pool), spare)
            holding[i] = holding[i] + more
            spare = spare - more
    return np.array([limit] + holding)


def ragged_sizes(own_key, amount, total, limit, skew):
    if amount == 2:
        one = jax.random.randint(own_key, (), max(1, total - limit), min(limit, total - 1) + 1)
        return jnp.stack([one, total - one])
    sizes = jnp.asarray(length_profile(amount, total, limit, skew), jnp.int32)
    pairs = (amount - 1) // 2
    donor, receiver = sizes[1:1 + 2 * pairs:2], sizes[2:2 + 2 * pairs:2]
    margin = jnp.minimum(donor - 1, limit - receiver)
    passed = jax.random.randint(jax.random.fold_in(own_key, 1), (pairs,), 0, 1 << 20) % (margin + 1)
    sizes = sizes.at[1:1 + 2 * pairs:2].set(donor - passed).at[2:2 + 2 * pairs:2].set(receiver + passed)
    return sizes[jax.random.permutation(jax.random.fold_in(own_key, 2), amount)]


def scatter_about(own_key, dims, spread, bound, cuts=(), kind=jnp.bfloat16):
    factor_of = level_of(own_key, dims, cuts, -0.22, 0.18) if cuts else 1.0
    result = jax.random.normal(own_key, dims, jnp.float32) * spread * factor_of
    return jnp.minimum(jnp.maximum(result, -bound), bound).astype(kind)


def setup_inputs(seed: int = 0, part: int = 0) -> dict:
    key_of = jax.random.split(jax.random.key(seed), 8)
    own_keys = jax.random.split(jax.random.fold_in(key_of[7], part), 8)
    rhs = scatter_about(own_keys[0], (NBR, N_PROW, BS, RHS), 1.0, 6.0, ((1, 32),))
    lower_factor_t = scatter_about(own_keys[1], (NBR, N_PROW, BS, NBR, N_PROW, BS), (8 * BS) ** -0.5, 0.1875, ((4, 32),))
    upper_factor_t = scatter_about(own_keys[2], (NBR, N_PROW, BS, NBR, N_PROW, BS), (8 * BS) ** -0.5, 0.1875, ((4, 32),))
    lower_snode = jnp.searchsorted(jnp.cumsum(ragged_sizes(own_keys[3], LCOUNT, LB, min(16, LB), 1)), jnp.arange(LB), side="right").astype(jnp.int32)
    upper_snode = jnp.searchsorted(jnp.cumsum(ragged_sizes(own_keys[4], UCOUNT, UB, min(16, UB), 1)), jnp.arange(UB), side="right").astype(jnp.int32)
    parent = different_ones(own_keys[5], LCOUNT, UCOUNT, 1, 0)
    pattern = set_ends((jax.random.randint(own_keys[6], (UB, LCOUNT), 0, 2) < 1).astype(jnp.int32), jax.random.fold_in(own_keys[6], 1), 0, 1)
    return dict(rhs=rhs, lower_factor_t=lower_factor_t, upper_factor_t=upper_factor_t, lower_snode=lower_snode, upper_snode=upper_snode, parent=parent, pattern=pattern)


def block_masks(lower_snode, upper_snode, parent, pattern):
    count_lower = parent.shape[0]
    snode_ids = jnp.concatenate([lower_snode, upper_snode + count_lower])
    same = snode_ids[:, None] == snode_ids[None, :]
    onehot = (lower_snode[:, None] == jnp.arange(count_lower, dtype=jnp.int32)[None, :]).astype(jnp.int32)
    parent_block = jnp.sum(onehot * parent[:, 0][None, :], axis=1)
    pattern_block = jnp.sum(pattern[:, None, :] * onehot[None, :, :], axis=2)
    link = (upper_snode[:, None] == parent_block[None, :]) & (pattern_block == 1)
    return same, link


def couplings(link):
    upper_count, lower_count = link.shape
    total = upper_count + lower_count
    couple_lower = jnp.concatenate([jnp.zeros((lower_count, total), bool), jnp.concatenate([link, jnp.zeros((upper_count, upper_count), bool)], 1)], 0)
    couple_upper = jnp.concatenate([jnp.concatenate([jnp.zeros((lower_count, lower_count), bool), link.T], 1), jnp.zeros((upper_count, total), bool)], 0)
    return couple_lower, couple_upper


def product(transposed, block_rule, tri, row_first, rows, col_first, cols, vector):
    step = BS * math.gcd(rows // BS, 16)
    pieces = []
    for start in range(row_first, row_first + rows, step):
        row_ids = start + jnp.arange(step, dtype=jnp.int32)
        col_ids = col_first + jnp.arange(cols, dtype=jnp.int32)
        allowed = block_rule[row_ids // BS][:, col_ids // BS]
        if tri > 0:
            allowed = allowed & (row_ids[:, None] >= col_ids[None, :])
        if tri < 0:
            allowed = allowed & (row_ids[:, None] <= col_ids[None, :])
        section = transposed[col_first:col_first + cols, start:start + step]
        kept = jnp.where(allowed.T, section, jnp.zeros((), section.dtype))
        pieces.append(jnp.dot(kept.T.astype(jnp.float32), vector.astype(jnp.float32), preferred_element_type=jnp.float32))
    return jnp.concatenate(pieces, 0)


def reference(rhs, lower_factor_t, upper_factor_t, lower_snode, upper_snode, parent, pattern):
    order = NB * BS
    width = rhs.shape[3]
    right = rhs.reshape(order, width)
    lower_t = lower_factor_t.reshape(order, order)
    upper_t = upper_factor_t.reshape(order, order)
    same, link = block_masks(lower_snode, upper_snode, parent, pattern)
    couple_lower, couple_upper = couplings(link)
    split = LB * BS
    rest = order - split
    forward_lower = product(lower_t, same, 1, 0, split, 0, split, right[:split])
    lower_known = forward_lower.astype(jnp.bfloat16)
    coupling = product(lower_t, couple_lower, 0, split, rest, 0, split, lower_known).astype(jnp.bfloat16)
    upper_direct = product(lower_t, same, 1, split, rest, split, rest, right[split:])
    upper_update = product(lower_t, same, 1, split, rest, split, rest, coupling)
    forward_upper = upper_direct - upper_update
    upper_known = forward_upper.astype(jnp.bfloat16)
    backward_upper = product(upper_t, same, -1, split, rest, split, rest, upper_known)
    back_known = backward_upper.astype(jnp.bfloat16)
    correction = product(upper_t, couple_upper, 0, 0, split, split, rest, back_known).astype(jnp.bfloat16)
    lower_direct = product(upper_t, same, -1, 0, split, 0, split, lower_known)
    lower_update = product(upper_t, same, -1, 0, split, 0, split, correction)
    backward_lower = lower_direct - lower_update
    forward_solution = jnp.concatenate([forward_lower, forward_upper], 0).reshape(NBR, N_PROW, BS, width)
    backward_solution = jnp.concatenate([backward_lower, backward_upper], 0).reshape(NBR, N_PROW, BS, width)
    return forward_solution, backward_solution
```

```python
import functools
import jax
import jax.numpy as jnp
from jax import lax
from jax.experimental import pallas as pl
from jax.experimental.pallas import tpu as pltpu
from jax.sharding import PartitionSpec as P

SPAN = 16
PLANE = 8
PLANES = 4
VMEM_BYTES = 48 * 1024 * 1024


def window_start(block, direction, count):
    if direction > 0:
        return jnp.maximum(block - (SPAN - 1), 0)
    return jnp.minimum(block, count - SPAN)


def keep_window(out, block, start, direction, snode, first):
    own = snode[block]

    def clear(step, carry):
        other = start + step
        if direction > 0:
            kept = (snode[other] == own) & (other <= block)
        else:
            kept = (snode[other] == own) & (other >= block)

        @pl.when(jnp.logical_not(kept))
        def _():
            out[first + step] = jnp.zeros(out.shape[1:], out.dtype)

        return carry

    lax.fori_loop(0, SPAN, clear, 0)
    size = out.shape[1]
    col = lax.broadcasted_iota(jnp.int32, (size, size), 0)
    row = lax.broadcasted_iota(jnp.int32, (size, size), 1)
    tri = row >= col if direction > 0 else row <= col
    diagonal = out[first + block - start]
    out[first + block - start] = jnp.where(tri, diagonal, jnp.zeros_like(diagonal))


def pack_level_kernel(direction, base, rows, row_first, count, factor, snode, out, sems):
    me = lax.axis_index("prow")
    copies = []
    for row in range(rows):
        block = row * PLANE * PLANES + me
        start = window_start(block, direction, count)
        copy = pltpu.make_async_copy(
            factor.at[pl.ds(base + start, SPAN), row_first + row],
            out.at[pl.ds(row * SPAN, SPAN)],
            sems.at[row],
        )
        copy.start()
        copies.append((copy, block, start))
    for row, (copy, block, start) in enumerate(copies):
        copy.wait()
        keep_window(out, block, start, direction, snode, row * SPAN)


def pack_level(factor, snode, direction, base, rows, row_first, count):
    size = factor.shape[-1]
    return pl.pallas_call(
        functools.partial(pack_level_kernel, direction, base, rows, row_first, count),
        out_shape=jax.ShapeDtypeStruct((rows * SPAN, size, size), factor.dtype),
        in_specs=[
            pl.BlockSpec(memory_space=pl.ANY),
            pl.BlockSpec(memory_space=pltpu.SMEM),
        ],
        out_specs=pl.BlockSpec(memory_space=pltpu.VMEM),
        scratch_shapes=[pltpu.SemaphoreType.DMA((rows,))],
        compiler_params=pltpu.CompilerParams(vmem_limit_bytes=VMEM_BYTES),
        cost_estimate=pl.CostEstimate(flops=0, bytes_accessed=4 * rows * SPAN * size * size, transcendentals=0),
        name="pack_level",
    )(factor, snode)


def pack_down_kernel(factor, lower_snode, upper_snode, parent, pattern, out, sem):
    me = lax.axis_index("prow")
    count = out.shape[0]
    copy = pltpu.make_async_copy(factor.at[pl.ds(0, count), 2], out, sem)
    copy.start()
    copy.wait()

    def clear(block, carry):
        child = lower_snode[block]
        linked = (parent[child, 0] == upper_snode[me]) & (pattern[me, child] == 1)

        @pl.when(jnp.logical_not(linked))
        def _():
            out[block] = jnp.zeros(out.shape[1:], out.dtype)

        return carry

    lax.fori_loop(0, count, clear, 0)


def pack_up_kernel(factor, lower_snode, upper_snode, parent, pattern, out, sems):
    me = lax.axis_index("prow")
    count = out.shape[1]
    copies = []
    for row in range(2):
        copy = pltpu.make_async_copy(
            factor.at[pl.ds(2 * count, count), row], out.at[row], sems.at[row]
        )
        copy.start()
        copies.append(copy)
    for row in range(2):
        copies[row].wait()
        child = lower_snode[row * count + me]
        above = parent[child, 0]

        def clear(block, carry):
            linked = (above == upper_snode[block]) & (pattern[block, child] == 1)

            @pl.when(jnp.logical_not(linked))
            def _():
                out[row, block] = jnp.zeros(out.shape[2:], out.dtype)

            return carry

        lax.fori_loop(0, count, clear, 0)


def pack_coupling(kernel, name, shape, sems, factor, *tables):
    return pl.pallas_call(
        kernel,
        out_shape=jax.ShapeDtypeStruct(shape, factor.dtype),
        in_specs=[pl.BlockSpec(memory_space=pl.ANY)]
        + [pl.BlockSpec(memory_space=pltpu.SMEM)] * 4,
        out_specs=pl.BlockSpec(memory_space=pltpu.VMEM),
        scratch_shapes=[sems],
        compiler_params=pltpu.CompilerParams(vmem_limit_bytes=VMEM_BYTES),
        cost_estimate=pl.CostEstimate(flops=0, bytes_accessed=4 * 64 * 128 * 128, transcendentals=0),
        name=name,
    )(factor, *tables)


def gather(block, shifts):
    total = PLANE * PLANES

    def move(value, pairs):
        return lax.ppermute(value, "prow", pairs)

    parts = [block[None]]
    for shift in shifts:
        if shift[0] == "xor":
            pairs = [(i, i ^ (PLANE * shift[1])) for i in range(total)]
        else:
            pairs = [(i, (i + PLANE * shift[1]) % total) for i in range(total)]
        parts.append(move(block[None], pairs))
    pieces = {0: jnp.concatenate(parts, 0)}
    for k in (6, 2, 4):
        pieces[k] = move(pieces[0], [(i, i ^ k) for i in range(total)])
    for k in (0, 6, 2, 4):
        pieces[k + 1] = move(pieces[k], [(i, i ^ 1) for i in range(total)])
    return [pieces[k] for k in range(PLANE)]


def copy_window(pieces, xs, block, start, direction):
    me = lax.axis_index("prow")
    offset = me & (PLANE - 1)
    size = xs.shape[0]
    for k in range(PLANE):
        other = offset ^ k
        first = (other - start) & (PLANE - 1)
        for half in range(SPAN // PLANE):
            slot = first + half * PLANE
            source = start + slot
            apart = direction * (block // PLANE - source // PLANE)
            apart = jnp.clip(apart, 0, 2)
            level = source // (PLANE * PLANES) if pieces[k].shape[1] > 1 else 0
            at = pl.multiple_of(slot * size, size)
            xs[:, pl.ds(at, size)] = pieces[k][apart, level]


def dot(left, right):
    return jnp.dot(left, right, preferred_element_type=jnp.float32)


def forward_lower_kernel(*refs):
    pieces, (factor, solved, known, xs) = refs[:PLANE], refs[PLANE:]
    me = lax.axis_index("prow")
    size = xs.shape[0]
    for row in range(2):
        block = row * PLANE * PLANES + me
        start = window_start(block, 1, 2 * PLANE * PLANES)
        copy_window(pieces, xs, block, start, 1)
        result = dot(xs[...], factor[row * SPAN : (row + 1) * SPAN].reshape(SPAN * size, size))
        solved[row] = result
        known[row] = result.astype(known.dtype)


def coupling_kernel(*refs):
    pieces, (factor, rhs, out, xs) = refs[:PLANE], refs[PLANE:]
    me = lax.axis_index("prow")
    offset, plane = me & (PLANE - 1), me // PLANE
    size = xs.shape[0]
    for k in range(PLANE):
        for along in range(PLANES):
            for row in range(2):
                source = row * PLANE * PLANES + (plane ^ along) * PLANE + (offset ^ k)
                xs[:, pl.ds(pl.multiple_of(source * size, size), size)] = pieces[k][along, row]
    result = dot(xs[...], factor[...].reshape(2 * PLANE * PLANES * size, size))
    out[0] = (rhs[2].astype(jnp.float32) - result).astype(out.dtype)


def upper_kernel(direction, *refs):
    pieces, (factor, solved, known, xs) = refs[:PLANE], refs[PLANE:]
    me = lax.axis_index("prow")
    size = xs.shape[0]
    start = window_start(me, direction, PLANE * PLANES)
    copy_window(pieces, xs, me, start, direction)
    result = dot(xs[...], factor[...].reshape(SPAN * size, size))
    solved[0] = result
    known[0] = result.astype(known.dtype)


def correction_kernel(*refs):
    pieces, (factor, solved, out, xs) = refs[:PLANE], refs[PLANE:]
    me = lax.axis_index("prow")
    offset, plane = me & (PLANE - 1), me // PLANE
    size = xs.shape[0]
    for k in range(PLANE):
        for along in range(PLANES):
            source = (plane ^ along) * PLANE + (offset ^ k)
            xs[:, pl.ds(pl.multiple_of(source * size, size), size)] = pieces[k][along, 0]
    for row in range(2):
        result = dot(xs[...], factor[row].reshape(PLANE * PLANES * size, size))
        known = solved[row].astype(out.dtype).astype(jnp.float32)
        out[row] = (known - result).astype(out.dtype)


def backward_lower_kernel(*refs):
    pieces, (factor, upper, out, xs) = refs[:PLANE], refs[PLANE:]
    me = lax.axis_index("prow")
    size = xs.shape[0]
    for row in range(2):
        block = row * PLANE * PLANES + me
        start = window_start(block, -1, 2 * PLANE * PLANES)
        copy_window(pieces, xs, block, start, -1)
        result = dot(xs[...], factor[row * SPAN : (row + 1) * SPAN].reshape(SPAN * size, size))
        out[row, 0] = result.T
    out[2, 0] = upper[0].T


def turn_kernel(value, out):
    for row in range(3):
        out[row] = value[row, 0].astype(jnp.float32).T.astype(out.dtype)


def forward_out_kernel(lower, upper, out):
    for row in range(2):
        out[row, 0] = lower[row].T
    out[2, 0] = upper[0].T


def local_call(kernel, name, shapes, operands, width=0, flops=0):
    size = 128
    scratch = [pltpu.VMEM((size, width), jnp.bfloat16)] if width else []
    outs = [jax.ShapeDtypeStruct(*shape) for shape in shapes]
    return pl.pallas_call(
        kernel,
        out_shape=outs,
        in_specs=[pl.BlockSpec(memory_space=pltpu.VMEM)] * len(operands),
        out_specs=[pl.BlockSpec(memory_space=pltpu.VMEM)] * len(outs),
        scratch_shapes=scratch,
        compiler_params=pltpu.CompilerParams(vmem_limit_bytes=VMEM_BYTES),
        cost_estimate=pl.CostEstimate(flops=flops, bytes_accessed=1 << 20, transcendentals=0),
        name=name,
    )(*operands)


def fast_device(rhs, lower_factor_t, upper_factor_t, lower_snode, upper_snode, parent, pattern):
    rows, _, size, width = rhs.shape
    total = PLANE * PLANES
    f32, bf16 = jnp.float32, jnp.bfloat16

    def blocks(factor):
        return jnp.transpose(factor, (0, 1, 3, 4, 2, 5)).reshape(rows * total, rows, size, size)

    lower, upper = blocks(lower_factor_t), blocks(upper_factor_t)
    tables = (lower_snode, upper_snode, parent, pattern)
    own = local_call(turn_kernel, "turn", [((rows, width, size), bf16)], [rhs])[0]

    forward = (("shift", 1), ("shift", 2))
    backward = (("shift", -1), ("shift", -2))
    whole = (("xor", 1), ("xor", 2), ("xor", 3))

    pieces = gather(own[:2], forward)
    pack_l1 = pack_level(lower, lower_snode, 1, 0, 2, 0, 2 * total)
    solved, known = local_call(
        forward_lower_kernel,
        "forward_lower",
        [((2, width, size), f32), ((2, width, size), bf16)],
        [*pieces, pack_l1],
        SPAN * size,
    )
    pieces = gather(known, whole)
    pack_c = pack_coupling(
        pack_down_kernel, "pack_down", (2 * total, size, size), pltpu.SemaphoreType.DMA, lower, *tables
    )
    (difference,) = local_call(
        coupling_kernel,
        "coupling",
        [((1, width, size), bf16)],
        [*pieces, pack_c, own],
        2 * total * size,
    )
    pieces = gather(difference, forward)
    pack_l2 = pack_level(lower, upper_snode, 1, 2 * total, 1, 2, total)
    forward_upper, upper_known = local_call(
        functools.partial(upper_kernel, 1),
        "forward_upper",
        [((1, width, size), f32), ((1, width, size), bf16)],
        [*pieces, pack_l2],
        SPAN * size,
    )
    pieces = gather(upper_known, backward)
    pack_u2 = pack_level(upper, upper_snode, -1, 2 * total, 1, 2, total)
    (forward_solution,) = local_call(
        forward_out_kernel,
        "forward_out",
        [((rows, 1, size, width), f32)],
        [solved, forward_upper],
    )
    backward_upper, back_known = local_call(
        functools.partial(upper_kernel, -1),
        "backward_upper",
        [((1, width, size), f32), ((1, width, size), bf16)],
        [*pieces, pack_u2],
        SPAN * size,
    )
    pieces = gather(back_known, whole)
    pack_k = pack_coupling(
        pack_up_kernel, "pack_up", (2, total, size, size), pltpu.SemaphoreType.DMA((2,)), upper, *tables
    )
    (remainder,) = local_call(
        correction_kernel,
        "correction",
        [((2, width, size), bf16)],
        [*pieces, pack_k, solved],
        total * size,
    )
    pieces = gather(remainder, backward)
    pack_u1 = pack_level(upper, lower_snode, -1, 0, 2, 0, 2 * total)
    (backward_solution,) = local_call(
        backward_lower_kernel,
        "backward_lower",
        [((rows, 1, size, width), f32)],
        [*pieces, pack_u1, backward_upper],
        SPAN * size,
    )
    return forward_solution, backward_solution


def block_masks(lower_snode, upper_snode, parent, pattern):
    count_lower = parent.shape[0]
    snode_ids = jnp.concatenate([lower_snode, upper_snode + count_lower])
    same = snode_ids[:, None] == snode_ids[None, :]
    onehot = (lower_snode[:, None] == jnp.arange(count_lower, dtype=jnp.int32)[None, :]).astype(
        jnp.int32
    )
    parent_block = jnp.sum(onehot * parent[:, 0][None, :], axis=1)
    pattern_block = jnp.sum(pattern[:, None, :] * onehot[None, :, :], axis=2)
    link = (upper_snode[:, None] == parent_block[None, :]) & (pattern_block == 1)
    return (same, link)


def couplings(link):
    upper_count, lower_count = link.shape
    total = upper_count + lower_count
    couple_lower = jnp.concatenate(
        [
            jnp.zeros((lower_count, total), bool),
            jnp.concatenate([link, jnp.zeros((upper_count, upper_count), bool)], 1),
        ],
        0,
    )
    couple_upper = jnp.concatenate(
        [
            jnp.concatenate([jnp.zeros((lower_count, lower_count), bool), link.T], 1),
            jnp.zeros((upper_count, total), bool),
        ],
        0,
    )
    return (couple_lower, couple_upper)


def on_device(rhs, lower_factor_t, upper_factor_t, lower_snode, upper_snode, parent, pattern):
    rows_axis = lax.axis_size("prow")
    row_index = lax.axis_index("prow")
    col_index = lax.axis_index("pcol")
    blocks_local = rhs.shape[0]
    sub_rows = rhs.shape[2]
    col_group = lower_factor_t.shape[1]
    block_size = lower_factor_t.shape[2]
    lower_local = lower_snode.shape[0] // rows_axis
    same, link = block_masks(lower_snode, upper_snode, parent, pattern)
    couple_lower, couple_upper = couplings(link)
    all_blocks = same.shape[0]

    def local_blocks(whole):
        selected = lax.dynamic_index_in_dim(
            whole.reshape(blocks_local, rows_axis, all_blocks), row_index, 1, keepdims=False
        )
        selected = selected.reshape(blocks_local, blocks_local, rows_axis)
        selected = lax.dynamic_slice_in_dim(selected, col_index * col_group, col_group, 2)
        return jnp.transpose(selected, (1, 2, 0)).reshape(
            blocks_local, col_group, 1, blocks_local, 1, 1
        )

    local_ids = jnp.arange(blocks_local, dtype=jnp.int32)
    row_elem = (
        (local_ids[:, None] * rows_axis + row_index) * block_size
        + jnp.arange(block_size, dtype=jnp.int32)[None, :]
    ).reshape(1, 1, 1, blocks_local, 1, block_size)
    own_cols = col_index * col_group + jnp.arange(col_group, dtype=jnp.int32)
    col_block = local_ids[:, None] * rows_axis + own_cols[None, :]
    col_elem = (
        col_block[:, :, None] * block_size + jnp.arange(block_size, dtype=jnp.int32)[None, None, :]
    ).reshape(blocks_local, col_group, block_size, 1, 1, 1)
    same_local = local_blocks(same)
    keep_lower = same_local & (row_elem >= col_elem) | local_blocks(couple_lower)
    keep_upper = same_local & (row_elem <= col_elem) | local_blocks(couple_upper)
    lower_kept = jnp.where(keep_lower, lower_factor_t, jnp.zeros((), lower_factor_t.dtype))
    upper_kept = jnp.where(keep_upper, upper_factor_t, jnp.zeros((), upper_factor_t.dtype))

    def apply_factor(factor, vector, col_range, row_range):
        window = factor[col_range[0] : col_range[1], :, :, row_range[0] : row_range[1], 0, :]
        pieces_in = lax.all_gather(vector, "prow", axis=1, tiled=True)
        selector = (
            jnp.arange(pieces_in.shape[1], dtype=jnp.int32)[:, None] == own_cols[None, :]
        ).astype(jnp.bfloat16)
        picked = jnp.einsum(
            "rjen,jq->rqen", pieces_in, selector, preferred_element_type=jnp.float32
        ).astype(jnp.bfloat16)
        summed = lax.dot_general(
            window, picked, (((0, 1, 2), (0, 1, 2)), ((), ())), preferred_element_type=jnp.float32
        )[:, None]
        return lax.psum(summed, "pcol")

    source = lax.all_gather(rhs, "pcol", axis=2, tiled=True)
    rhs_width = source.shape[3]
    lower_span = (0, lower_local)
    upper_span = (lower_local, blocks_local)
    rhs_lower = source[:lower_local]
    rhs_upper = source[lower_local:]
    forward_lower = apply_factor(lower_kept, rhs_lower, lower_span, lower_span)
    lower_known = forward_lower.astype(jnp.bfloat16)
    coupling = apply_factor(lower_kept, lower_known, lower_span, upper_span).astype(jnp.bfloat16)
    joined = apply_factor(
        lower_kept, jnp.concatenate([rhs_upper, coupling], 3), upper_span, upper_span
    )
    upper_direct = joined[..., :rhs_width]
    upper_update = joined[..., rhs_width:]
    forward_upper = upper_direct - upper_update
    upper_known = forward_upper.astype(jnp.bfloat16)
    backward_upper = apply_factor(upper_kept, upper_known, upper_span, upper_span)
    back_known = backward_upper.astype(jnp.bfloat16)
    correction = apply_factor(upper_kept, back_known, upper_span, lower_span).astype(jnp.bfloat16)
    joined_lower = apply_factor(
        upper_kept, jnp.concatenate([lower_known, correction], 3), lower_span, lower_span
    )
    lower_direct = joined_lower[..., :rhs_width]
    lower_update = joined_lower[..., rhs_width:]
    backward_lower = lower_direct - lower_update
    forward_solution = jnp.concatenate([forward_lower, forward_upper], 0)
    backward_solution = jnp.concatenate([backward_lower, backward_upper], 0)
    forward_solution = lax.dynamic_slice_in_dim(forward_solution, col_index * sub_rows, sub_rows, 2)
    backward_solution = lax.dynamic_slice_in_dim(
        backward_solution, col_index * sub_rows, sub_rows, 2
    )
    return (forward_solution, backward_solution)


def solution(mesh):
    placed = (
        P("parts", "prow", "pcol", None),
        P("parts", "pcol", None, None, "prow", None),
        P("parts", "pcol", None, None, "prow", None),
        P("parts"),
        P("parts"),
        P("parts", None),
        P("parts", None),
    )
    total = PLANE * PLANES
    simple = mesh.shape["prow"] == total and mesh.shape["pcol"] == 1
    return jax.shard_map(
        fast_device if simple else on_device,
        mesh=mesh,
        in_specs=placed,
        out_specs=(P("parts", "prow", "pcol", None), P("parts", "prow", "pcol", None)),
        check_vma=False,
    )
```

```python
import functools
import jax
import jax.numpy as jnp
from jax import lax
from jax.experimental import pallas as pl
from jax.experimental.pallas import tpu as pltpu
from jax.sharding import PartitionSpec as P

SPAN = 16
PLANE = 8
PLANES = 4
VMEM_BYTES = 48 * 1024 * 1024


def window_start(block, direction, count):
    if direction > 0:
        return jnp.maximum(block - (SPAN - 1), 0)
    return jnp.minimum(block, count - SPAN)


def keep_window(out, block, start, direction, snode, first):
    own = snode[block]

    def clear(step, carry):
        other = start + step
        if direction > 0:
            kept = (snode[other] == own) & (other <= block)
        else:
            kept = (snode[other] == own) & (other >= block)

        @pl.when(jnp.logical_not(kept))
        def _():
            out[first + step] = jnp.zeros(out.shape[1:], out.dtype)

        return carry

    lax.fori_loop(0, SPAN, clear, 0)
    size = out.shape[1]
    col = lax.broadcasted_iota(jnp.int32, (size, size), 0)
    row = lax.broadcasted_iota(jnp.int32, (size, size), 1)
    tri = row >= col if direction > 0 else row <= col
    diagonal = out[first + block - start]
    out[first + block - start] = jnp.where(tri, diagonal, jnp.zeros_like(diagonal))


def pack_level_kernel(direction, base, rows, row_first, count, factor, snode, out, sems):
    me = lax.axis_index("prow")
    copies = []
    for row in range(rows):
        block = row * PLANE * PLANES + me
        start = window_start(block, direction, count)
        copy = pltpu.make_async_copy(
            factor.at[pl.ds(base + start, SPAN), row_first + row],
            out.at[pl.ds(row * SPAN, SPAN)],
            sems.at[row],
        )
        copy.start()
        copies.append((copy, block, start))
    for row, (copy, block, start) in enumerate(copies):
        copy.wait()
        keep_window(out, block, start, direction, snode, row * SPAN)


def pack_level(factor, snode, direction, base, rows, row_first, count):
    size = factor.shape[-1]
    return pl.pallas_call(
        functools.partial(pack_level_kernel, direction, base, rows, row_first, count),
        out_shape=jax.ShapeDtypeStruct((rows * SPAN, size, size), factor.dtype),
        in_specs=[
            pl.BlockSpec(memory_space=pl.ANY),
            pl.BlockSpec(memory_space=pltpu.SMEM),
        ],
        out_specs=pl.BlockSpec(memory_space=pltpu.VMEM),
        scratch_shapes=[pltpu.SemaphoreType.DMA((rows,))],
        compiler_params=pltpu.CompilerParams(vmem_limit_bytes=VMEM_BYTES),
        cost_estimate=pl.CostEstimate(flops=0, bytes_accessed=4 * rows * SPAN * size * size, transcendentals=0),
        name="pack_level",
    )(factor, snode)


def pack_down_kernel(factor, lower_snode, upper_snode, parent, pattern, out, sem):
    me = lax.axis_index("prow")
    count = out.shape[0]
    copy = pltpu.make_async_copy(factor.at[pl.ds(0, count), 2], out, sem)
    copy.start()
    copy.wait()

    def clear(block, carry):
        child = lower_snode[block]
        linked = (parent[child, 0] == upper_snode[me]) & (pattern[me, child] == 1)

        @pl.when(jnp.logical_not(linked))
        def _():
            out[block] = jnp.zeros(out.shape[1:], out.dtype)

        return carry

    lax.fori_loop(0, count, clear, 0)


def pack_up_kernel(factor, lower_snode, upper_snode, parent, pattern, out, sems):
    me = lax.axis_index("prow")
    count = out.shape[1]
    copies = []
    for row in range(2):
        copy = pltpu.make_async_copy(
            factor.at[pl.ds(2 * count, count), row], out.at[row], sems.at[row]
        )
        copy.start()
        copies.append(copy)
    for row in range(2):
        copies[row].wait()
        child = lower_snode[row * count + me]
        above = parent[child, 0]

        def clear(block, carry):
            linked = (above == upper_snode[block]) & (pattern[block, child] == 1)

            @pl.when(jnp.logical_not(linked))
            def _():
                out[row, block] = jnp.zeros(out.shape[2:], out.dtype)

            return carry

        lax.fori_loop(0, count, clear, 0)


def pack_coupling(kernel, name, shape, sems, factor, *tables):
    return pl.pallas_call(
        kernel,
        out_shape=jax.ShapeDtypeStruct(shape, factor.dtype),
        in_specs=[pl.BlockSpec(memory_space=pl.ANY)]
        + [pl.BlockSpec(memory_space=pltpu.SMEM)] * 4,
        out_specs=pl.BlockSpec(memory_space=pltpu.VMEM),
        scratch_shapes=[sems],
        compiler_params=pltpu.CompilerParams(vmem_limit_bytes=VMEM_BYTES),
        cost_estimate=pl.CostEstimate(flops=0, bytes_accessed=4 * 64 * 128 * 128, transcendentals=0),
        name=name,
    )(factor, *tables)


def gather(block, shifts, table, pack):
    total = PLANE * PLANES

    def move(value, pairs):
        return lax.ppermute(value, "prow", pairs)

    parts = [block[None]]
    for shift in shifts:
        if shift[0] == "xor":
            pairs = [(i, i ^ (PLANE * shift[1])) for i in range(total)]
        else:
            pairs = [(i, (i + PLANE * shift[1]) % total) for i in range(total)]
        parts.append(move(block[None], pairs))
    packed = pack(lax.optimization_barrier((table, block))[0])
    stacked, packed = lax.optimization_barrier((jnp.concatenate(parts, 0), packed))
    pieces = {0: stacked}
    for k in (6, 2, 4):
        pieces[k] = move(pieces[0], [(i, i ^ k) for i in range(total)])
    for k in (0, 6, 2, 4):
        pieces[k + 1] = move(pieces[k], [(i, i ^ 1) for i in range(total)])
    return [pieces[k] for k in range(PLANE)], packed


def copy_window(pieces, xs, block, start, direction):
    me = lax.axis_index("prow")
    offset = me & (PLANE - 1)
    size = xs.shape[0]
    for k in range(PLANE):
        other = offset ^ k
        first = (other - start) & (PLANE - 1)
        for half in range(SPAN // PLANE):
            slot = first + half * PLANE
            source = start + slot
            apart = direction * (block // PLANE - source // PLANE)
            apart = jnp.clip(apart, 0, 2)
            level = source // (PLANE * PLANES) if pieces[k].shape[1] > 1 else 0
            at = pl.multiple_of(slot * size, size)
            xs[:, pl.ds(at, size)] = pieces[k][apart, level]


def dot(left, right):
    return jnp.dot(left, right, preferred_element_type=jnp.float32)


def forward_lower_kernel(*refs):
    pieces, (factor, solved, known, xs) = refs[:PLANE], refs[PLANE:]
    me = lax.axis_index("prow")
    size = xs.shape[0]
    for row in range(2):
        block = row * PLANE * PLANES + me
        start = window_start(block, 1, 2 * PLANE * PLANES)
        copy_window(pieces, xs, block, start, 1)
        result = dot(xs[...], factor[row * SPAN : (row + 1) * SPAN].reshape(SPAN * size, size))
        solved[row] = result
        known[row] = result.astype(known.dtype)


def coupling_kernel(*refs):
    pieces, (factor, rhs, out, xs) = refs[:PLANE], refs[PLANE:]
    me = lax.axis_index("prow")
    offset, plane = me & (PLANE - 1), me // PLANE
    size = xs.shape[0]
    for k in range(PLANE):
        for along in range(PLANES):
            for row in range(2):
                source = row * PLANE * PLANES + (plane ^ along) * PLANE + (offset ^ k)
                xs[:, pl.ds(pl.multiple_of(source * size, size), size)] = pieces[k][along, row]
    result = dot(xs[...], factor[...].reshape(2 * PLANE * PLANES * size, size))
    rounded = result.astype(out.dtype).astype(jnp.float32)
    out[0] = (rhs[2].astype(jnp.float32) - rounded).astype(out.dtype)


def upper_kernel(direction, *refs):
    pieces, (factor, solved, known, xs) = refs[:PLANE], refs[PLANE:]
    me = lax.axis_index("prow")
    size = xs.shape[0]
    start = window_start(me, direction, PLANE * PLANES)
    copy_window(pieces, xs, me, start, direction)
    result = dot(xs[...], factor[...].reshape(SPAN * size, size))
    solved[0] = result
    known[0] = result.astype(known.dtype)


def correction_kernel(*refs):
    pieces, (factor, solved, out, xs) = refs[:PLANE], refs[PLANE:]
    me = lax.axis_index("prow")
    offset, plane = me & (PLANE - 1), me // PLANE
    size = xs.shape[0]
    for k in range(PLANE):
        for along in range(PLANES):
            source = (plane ^ along) * PLANE + (offset ^ k)
            xs[:, pl.ds(pl.multiple_of(source * size, size), size)] = pieces[k][along, 0]
    for row in range(2):
        result = dot(xs[...], factor[row].reshape(PLANE * PLANES * size, size))
        known = solved[row].astype(out.dtype).astype(jnp.float32)
        rounded = result.astype(out.dtype).astype(jnp.float32)
        out[row] = (known - rounded).astype(out.dtype)


def backward_lower_kernel(*refs):
    pieces, (factor, upper, out, xs) = refs[:PLANE], refs[PLANE:]
    me = lax.axis_index("prow")
    size = xs.shape[0]
    for row in range(2):
        block = row * PLANE * PLANES + me
        start = window_start(block, -1, 2 * PLANE * PLANES)
        copy_window(pieces, xs, block, start, -1)
        result = dot(xs[...], factor[row * SPAN : (row + 1) * SPAN].reshape(SPAN * size, size))
        out[row, 0] = result.T
    out[2, 0] = upper[0].T


def turn_kernel(value, out):
    for row in range(3):
        out[row] = value[row, 0].astype(jnp.float32).T.astype(out.dtype)


def forward_out_kernel(lower, upper, out):
    for row in range(2):
        out[row, 0] = lower[row].T
    out[2, 0] = upper[0].T


def local_call(kernel, name, shapes, operands, width=0, flops=0):
    size = 128
    scratch = [pltpu.VMEM((size, width), jnp.bfloat16)] if width else []
    outs = [jax.ShapeDtypeStruct(*shape) for shape in shapes]
    return pl.pallas_call(
        kernel,
        out_shape=outs,
        in_specs=[pl.BlockSpec(memory_space=pltpu.VMEM)] * len(operands),
        out_specs=[pl.BlockSpec(memory_space=pltpu.VMEM)] * len(outs),
        scratch_shapes=scratch,
        compiler_params=pltpu.CompilerParams(vmem_limit_bytes=VMEM_BYTES),
        cost_estimate=pl.CostEstimate(flops=flops, bytes_accessed=1 << 20, transcendentals=0),
        name=name,
    )(*operands)


def fast_device(rhs, lower_factor_t, upper_factor_t, lower_snode, upper_snode, parent, pattern):
    rows, _, size, width = rhs.shape
    total = PLANE * PLANES
    f32, bf16 = jnp.float32, jnp.bfloat16

    def blocks(factor):
        return jnp.transpose(factor, (0, 1, 3, 4, 2, 5)).reshape(rows * total, rows, size, size)

    lower, upper = blocks(lower_factor_t), blocks(upper_factor_t)
    tables = (lower_snode, upper_snode, parent, pattern)
    own = local_call(turn_kernel, "turn", [((rows, width, size), bf16)], [rhs])[0]

    forward = (("shift", 1), ("shift", 2))
    backward = (("shift", -1), ("shift", -2))
    whole = (("xor", 1), ("xor", 2), ("xor", 3))

    def pack_l1(table):
        return pack_level(lower, table, 1, 0, 2, 0, 2 * total)

    def pack_c(table):
        return pack_coupling(
            pack_down_kernel,
            "pack_down",
            (2 * total, size, size),
            pltpu.SemaphoreType.DMA,
            lower,
            table,
            *tables[1:],
        )

    def pack_l2(table):
        return pack_level(lower, table, 1, 2 * total, 1, 2, total)

    def pack_u2(table):
        return pack_level(upper, table, -1, 2 * total, 1, 2, total)

    def pack_k(table):
        return pack_coupling(
            pack_up_kernel,
            "pack_up",
            (2, total, size, size),
            pltpu.SemaphoreType.DMA((2,)),
            upper,
            table,
            *tables[1:],
        )

    def pack_u1(table):
        return pack_level(upper, table, -1, 0, 2, 0, 2 * total)

    pieces, packed = gather(own[:2], forward, lower_snode, pack_l1)
    solved, known = local_call(
        forward_lower_kernel,
        "forward_lower",
        [((2, width, size), f32), ((2, width, size), bf16)],
        [*pieces, packed],
        SPAN * size,
    )
    pieces, packed = gather(known, whole, lower_snode, pack_c)
    (difference,) = local_call(
        coupling_kernel,
        "coupling",
        [((1, width, size), bf16)],
        [*pieces, packed, own],
        2 * total * size,
    )
    pieces, packed = gather(difference, forward, upper_snode, pack_l2)
    forward_upper, upper_known = local_call(
        functools.partial(upper_kernel, 1),
        "forward_upper",
        [((1, width, size), f32), ((1, width, size), bf16)],
        [*pieces, packed],
        SPAN * size,
    )
    pieces, packed = gather(upper_known, backward, upper_snode, pack_u2)
    (forward_solution,) = local_call(
        forward_out_kernel,
        "forward_out",
        [((rows, 1, size, width), f32)],
        [solved, forward_upper],
    )
    backward_upper, back_known = local_call(
        functools.partial(upper_kernel, -1),
        "backward_upper",
        [((1, width, size), f32), ((1, width, size), bf16)],
        [*pieces, packed],
        SPAN * size,
    )
    pieces, packed = gather(back_known, whole, lower_snode, pack_k)
    (remainder,) = local_call(
        correction_kernel,
        "correction",
        [((2, width, size), bf16)],
        [*pieces, packed, solved],
        total * size,
    )
    pieces, packed = gather(remainder, backward, lower_snode, pack_u1)
    (backward_solution,) = local_call(
        backward_lower_kernel,
        "backward_lower",
        [((rows, 1, size, width), f32)],
        [*pieces, packed, backward_upper],
        SPAN * size,
    )
    return forward_solution, backward_solution


def block_masks(lower_snode, upper_snode, parent, pattern):
    count_lower = parent.shape[0]
    snode_ids = jnp.concatenate([lower_snode, upper_snode + count_lower])
    same = snode_ids[:, None] == snode_ids[None, :]
    onehot = (lower_snode[:, None] == jnp.arange(count_lower, dtype=jnp.int32)[None, :]).astype(
        jnp.int32
    )
    parent_block = jnp.sum(onehot * parent[:, 0][None, :], axis=1)
    pattern_block = jnp.sum(pattern[:, None, :] * onehot[None, :, :], axis=2)
    link = (upper_snode[:, None] == parent_block[None, :]) & (pattern_block == 1)
    return (same, link)


def couplings(link):
    upper_count, lower_count = link.shape
    total = upper_count + lower_count
    couple_lower = jnp.concatenate(
        [
            jnp.zeros((lower_count, total), bool),
            jnp.concatenate([link, jnp.zeros((upper_count, upper_count), bool)], 1),
        ],
        0,
    )
    couple_upper = jnp.concatenate(
        [
            jnp.concatenate([jnp.zeros((lower_count, lower_count), bool), link.T], 1),
            jnp.zeros((upper_count, total), bool),
        ],
        0,
    )
    return (couple_lower, couple_upper)


def on_device(rhs, lower_factor_t, upper_factor_t, lower_snode, upper_snode, parent, pattern):
    rows_axis = lax.axis_size("prow")
    row_index = lax.axis_index("prow")
    col_index = lax.axis_index("pcol")
    blocks_local = rhs.shape[0]
    sub_rows = rhs.shape[2]
    col_group = lower_factor_t.shape[1]
    block_size = lower_factor_t.shape[2]
    lower_local = lower_snode.shape[0] // rows_axis
    same, link = block_masks(lower_snode, upper_snode, parent, pattern)
    couple_lower, couple_upper = couplings(link)
    all_blocks = same.shape[0]

    def local_blocks(whole):
        selected = lax.dynamic_index_in_dim(
            whole.reshape(blocks_local, rows_axis, all_blocks), row_index, 1, keepdims=False
        )
        selected = selected.reshape(blocks_local, blocks_local, rows_axis)
        selected = lax.dynamic_slice_in_dim(selected, col_index * col_group, col_group, 2)
        return jnp.transpose(selected, (1, 2, 0)).reshape(
            blocks_local, col_group, 1, blocks_local, 1, 1
        )

    local_ids = jnp.arange(blocks_local, dtype=jnp.int32)
    row_elem = (
        (local_ids[:, None] * rows_axis + row_index) * block_size
        + jnp.arange(block_size, dtype=jnp.int32)[None, :]
    ).reshape(1, 1, 1, blocks_local, 1, block_size)
    own_cols = col_index * col_group + jnp.arange(col_group, dtype=jnp.int32)
    col_block = local_ids[:, None] * rows_axis + own_cols[None, :]
    col_elem = (
        col_block[:, :, None] * block_size + jnp.arange(block_size, dtype=jnp.int32)[None, None, :]
    ).reshape(blocks_local, col_group, block_size, 1, 1, 1)
    same_local = local_blocks(same)
    keep_lower = same_local & (row_elem >= col_elem) | local_blocks(couple_lower)
    keep_upper = same_local & (row_elem <= col_elem) | local_blocks(couple_upper)
    lower_kept = jnp.where(keep_lower, lower_factor_t, jnp.zeros((), lower_factor_t.dtype))
    upper_kept = jnp.where(keep_upper, upper_factor_t, jnp.zeros((), upper_factor_t.dtype))

    def apply_factor(factor, vector, col_range, row_range):
        window = factor[col_range[0] : col_range[1], :, :, row_range[0] : row_range[1], 0, :]
        pieces_in = lax.all_gather(vector, "prow", axis=1, tiled=True)
        selector = (
            jnp.arange(pieces_in.shape[1], dtype=jnp.int32)[:, None] == own_cols[None, :]
        ).astype(jnp.bfloat16)
        picked = jnp.einsum(
            "rjen,jq->rqen", pieces_in, selector, preferred_element_type=jnp.float32
        ).astype(jnp.bfloat16)
        summed = lax.dot_general(
            window, picked, (((0, 1, 2), (0, 1, 2)), ((), ())), preferred_element_type=jnp.float32
        )[:, None]
        return lax.psum(summed, "pcol")

    source = lax.all_gather(rhs, "pcol", axis=2, tiled=True)
    rhs_width = source.shape[3]
    lower_span = (0, lower_local)
    upper_span = (lower_local, blocks_local)
    rhs_lower = source[:lower_local]
    rhs_upper = source[lower_local:]
    forward_lower = apply_factor(lower_kept, rhs_lower, lower_span, lower_span)
    lower_known = forward_lower.astype(jnp.bfloat16)
    coupling = apply_factor(lower_kept, lower_known, lower_span, upper_span).astype(jnp.bfloat16)
    joined = apply_factor(
        lower_kept, jnp.concatenate([rhs_upper, coupling], 3), upper_span, upper_span
    )
    upper_direct = joined[..., :rhs_width]
    upper_update = joined[..., rhs_width:]
    forward_upper = upper_direct - upper_update
    upper_known = forward_upper.astype(jnp.bfloat16)
    backward_upper = apply_factor(upper_kept, upper_known, upper_span, upper_span)
    back_known = backward_upper.astype(jnp.bfloat16)
    correction = apply_factor(upper_kept, back_known, upper_span, lower_span).astype(jnp.bfloat16)
    joined_lower = apply_factor(
        upper_kept, jnp.concatenate([lower_known, correction], 3), lower_span, lower_span
    )
    lower_direct = joined_lower[..., :rhs_width]
    lower_update = joined_lower[..., rhs_width:]
    backward_lower = lower_direct - lower_update
    forward_solution = jnp.concatenate([forward_lower, forward_upper], 0)
    backward_solution = jnp.concatenate([backward_lower, backward_upper], 0)
    forward_solution = lax.dynamic_slice_in_dim(forward_solution, col_index * sub_rows, sub_rows, 2)
    backward_solution = lax.dynamic_slice_in_dim(
        backward_solution, col_index * sub_rows, sub_rows, 2
    )
    return (forward_solution, backward_solution)


def solution(mesh):
    placed = (
        P("parts", "prow", "pcol", None),
        P("parts", "pcol", None, None, "prow", None),
        P("parts", "pcol", None, None, "prow", None),
        P("parts"),
        P("parts"),
        P("parts", None),
        P("parts", None),
    )
    total = PLANE * PLANES
    simple = mesh.shape["prow"] == total and mesh.shape["pcol"] == 1
    return jax.shard_map(
        fast_device if simple else on_device,
        mesh=mesh,
        in_specs=placed,
        out_specs=(P("parts", "prow", "pcol", None), P("parts", "prow", "pcol", None)),
        check_vma=False,
    )
```

```python
import functools
import math
import jax
import jax.numpy as jnp
from jax import lax
from jax.experimental import pallas as pl
from jax.experimental.pallas import tpu as pltpu
from jax.sharding import PartitionSpec as P

SPAN = 16
PLANE = 8
PLANES = 4
VMEM_BYTES = 48 * 1024 * 1024


def window_start(block, direction, count):
    if direction > 0:
        return jnp.maximum(block - (SPAN - 1), 0)
    return jnp.minimum(block, count - SPAN)


def first_pair(start, parity):
    return (start + 1 - parity) // 2


def pack_level_kernel(direction, base, rows, row_first, count, factor, snode, mine, other, sems):
    me = lax.axis_index("prow")
    core = me & 1
    half = SPAN // 2
    copies = []
    for row in range(rows):
        block = row * PLANE * PLANES + me
        start = window_start(block, direction, count)
        for side, out in ((0, mine), (1, other)):
            parity = core ^ side
            pair = first_pair(start, parity)
            copy = pltpu.make_async_copy(
                factor.at[pl.ds(base // 2 + pair, half), parity, row_first + row],
                out.at[pl.ds(row * half, half)],
                sems.at[2 * row + side],
            )
            copy.start()
            copies.append((copy, row, block, pair, parity, out))
    for copy, row, block, pair, parity, out in copies:
        copy.wait()
        own = snode[block]
        for step in range(half):
            column = 2 * (pair + step) + parity
            if direction > 0:
                kept = (snode[column] == own) & (column <= block)
            else:
                kept = (snode[column] == own) & (column >= block)

            @pl.when(jnp.logical_not(kept))
            def _():
                out[row * half + step] = jnp.zeros(out.shape[1:], out.dtype)

        if out is mine:
            size = out.shape[1]
            col = lax.broadcasted_iota(jnp.int32, (size, size), 0)
            line = lax.broadcasted_iota(jnp.int32, (size, size), 1)
            tri = line >= col if direction > 0 else line <= col
            at = row * half + block // 2 - pair
            diagonal = out[at]
            out[at] = jnp.where(tri, diagonal, jnp.zeros_like(diagonal))


def pack_down_kernel(factor, lower_snode, upper_snode, parent, pattern, mine, other, sems):
    me = lax.axis_index("prow")
    core = me & 1
    count = mine.shape[0]
    copies = []
    for side, out in ((0, mine), (1, other)):
        copy = pltpu.make_async_copy(
            factor.at[pl.ds(0, count), core ^ side, 2], out, sems.at[side]
        )
        copy.start()
        copies.append(copy)
    for side, out in ((0, mine), (1, other)):
        copies[side].wait()

        def clear(pair, carry):
            child = lower_snode[2 * pair + (core ^ side)]
            linked = (parent[child, 0] == upper_snode[me]) & (pattern[me, child] == 1)

            @pl.when(jnp.logical_not(linked))
            def _():
                out[pair] = jnp.zeros(out.shape[1:], out.dtype)

            return carry

        lax.fori_loop(0, count, clear, 0)


def pack_up_kernel(factor, lower_snode, upper_snode, parent, pattern, mine, other, sems):
    me = lax.axis_index("prow")
    core = me & 1
    count = mine.shape[1]
    copies = []
    for side, out in ((0, mine), (1, other)):
        for row in range(2):
            copy = pltpu.make_async_copy(
                factor.at[pl.ds(2 * count, count), core ^ side, row],
                out.at[row],
                sems.at[2 * side + row],
            )
            copy.start()
            copies.append(copy)
    for side, out in ((0, mine), (1, other)):
        for row in range(2):
            copies[2 * side + row].wait()
            child = lower_snode[row * PLANE * PLANES + me]
            above = parent[child, 0]

            def clear(pair, carry):
                block = 2 * pair + (core ^ side)
                linked = (above == upper_snode[block]) & (pattern[block, child] == 1)

                @pl.when(jnp.logical_not(linked))
                def _():
                    out[row, pair] = jnp.zeros(out.shape[2:], out.dtype)

                return carry

            lax.fori_loop(0, count, clear, 0)


def pack_call(kernel, name, shape, copies, factor, *tables):
    return pl.pallas_call(
        kernel,
        out_shape=[jax.ShapeDtypeStruct(shape, factor.dtype)] * 2,
        in_specs=[pl.BlockSpec(memory_space=pl.ANY)]
        + [pl.BlockSpec(memory_space=pltpu.SMEM)] * len(tables),
        out_specs=[pl.BlockSpec(memory_space=pltpu.VMEM)] * 2,
        scratch_shapes=[pltpu.SemaphoreType.DMA((copies,))],
        compiler_params=pltpu.CompilerParams(vmem_limit_bytes=VMEM_BYTES),
        cost_estimate=pl.CostEstimate(
            flops=0, bytes_accessed=4 * factor.dtype.itemsize * math.prod(shape), transcendentals=0
        ),
        name=name,
    )(factor, *tables)


def swap(value, distance):
    return lax.ppermute(
        value, "prow", [(i, i ^ distance) for i in range(PLANE * PLANES)]
    )


def gather(block, direction, table, pack):
    total = PLANE * PLANES
    parts = [block[None]]
    if direction == 0:
        parts += [swap(block[None], PLANE * step) for step in range(1, PLANES)]
    else:
        for step in (1, 2):
            pairs = [(i, (i + direction * step * PLANE) % total) for i in range(total)]
            parts.append(lax.ppermute(block[None], "prow", pairs))
    mine, other = pack(lax.optimization_barrier((table, block))[0])
    parts, mine, other = lax.optimization_barrier((parts, mine, other))
    pieces = [jnp.concatenate(parts, 0)]
    me = lax.axis_index("prow")
    for k in (2, 4, 6):
        if direction == 0:
            sent = pieces[0]
        else:
            near, far = jnp.concatenate(parts[:2], 0), jnp.concatenate(parts[1:], 0)
            after = (me & (2 if k == 2 else 4)) != 0
            sent = jnp.where(after if direction > 0 else jnp.logical_not(after), far, near)
        pieces.append(swap(sent, k))
    return pieces, mine, swap(other, 1)


def copy_window(pieces, xs, block, start, direction):
    me = lax.axis_index("prow")
    offset, core = me & (PLANE - 1), me & 1
    size = xs.shape[0]
    lines = PLANE // 2
    pair = first_pair(start, core)
    for k, piece in zip((0, 2, 4, 6), pieces, strict=True):
        other = offset ^ k
        first = (other // 2 - pair) & (lines - 1)
        if k == 0:
            skipped = 0
        elif direction > 0:
            skipped = (other > offset).astype(jnp.int32)
        else:
            skipped = (other < offset).astype(jnp.int32)
        for half in range(2):
            slot = first + half * lines
            source = 2 * (pair + slot) + core
            apart = direction * (block // PLANE - source // PLANE) - skipped
            apart = jnp.clip(apart, 0, piece.shape[0] - 1)
            level = source // (PLANE * PLANES) if piece.shape[1] > 1 else 0
            at = pl.multiple_of(slot * size, size)
            xs[:, pl.ds(at, size)] = piece[apart, level]


def copy_all(pieces, xs):
    me = lax.axis_index("prow")
    offset, plane = me & (PLANE - 1), me // PLANE
    size = xs.shape[0]
    for k, piece in zip((0, 2, 4, 6), pieces, strict=True):
        for along in range(PLANES):
            for row in range(piece.shape[1]):
                pair = (row * PLANES + (plane ^ along)) * (PLANE // 2) + (offset ^ k) // 2
                xs[:, pl.ds(pl.multiple_of(pair * size, size), size)] = piece[along, row]


def dot(left, right):
    return jnp.dot(left, right, preferred_element_type=jnp.float32)


def window_kernel(direction, flip, *refs):
    pieces, (factor, out, xs) = refs[:4], refs[4:]
    me = lax.axis_index("prow") ^ flip
    size = xs.shape[0]
    rows, half = out.shape[0], SPAN // 2
    for row in range(rows):
        block = row * PLANE * PLANES + me
        start = window_start(block, direction, rows * PLANE * PLANES)
        copy_window(pieces, xs, block, start, direction)
        out[row] = dot(xs[...], factor[row * half : (row + 1) * half].reshape(half * size, size))


def down_kernel(*refs):
    pieces, (factor, out, xs) = refs[:4], refs[4:]
    copy_all(pieces, xs)
    out[0] = dot(xs[...], factor[...].reshape(xs.shape[1], xs.shape[0]))


def up_kernel(*refs):
    pieces, (factor, out, xs) = refs[:4], refs[4:]
    copy_all(pieces, xs)
    for row in range(out.shape[0]):
        out[row] = dot(xs[...], factor[row].reshape(xs.shape[1], xs.shape[0]))


def backward_out_kernel(mine, brought, upper, out):
    for row in range(2):
        out[row, 0] = (mine[row] + brought[row]).T
    out[2, 0] = upper[0].T


def turn_kernel(value, out):
    for row in range(3):
        out[row] = value[row, 0].astype(jnp.float32).T.astype(out.dtype)


def forward_out_kernel(lower, upper, out):
    for row in range(2):
        out[row, 0] = lower[row].T
    out[2, 0] = upper[0].T


def local_call(kernel, name, shape, dtype, operands, width=0):
    scratch = [pltpu.VMEM((shape[-2], width), jnp.bfloat16)] if width else []
    return pl.pallas_call(
        kernel,
        out_shape=jax.ShapeDtypeStruct(shape, dtype),
        in_specs=[pl.BlockSpec(memory_space=pltpu.VMEM)] * len(operands),
        out_specs=pl.BlockSpec(memory_space=pltpu.VMEM),
        scratch_shapes=scratch,
        compiler_params=pltpu.CompilerParams(vmem_limit_bytes=VMEM_BYTES),
        cost_estimate=pl.CostEstimate(flops=0, bytes_accessed=1 << 20, transcendentals=0),
        name=name,
    )(*operands)


def fast_device(rhs, lower_factor_t, upper_factor_t, lower_snode, upper_snode, parent, pattern):
    rows, _, size, width = rhs.shape
    total = PLANE * PLANES
    half = SPAN // 2
    f32, bf16 = jnp.float32, jnp.bfloat16

    def blocks(factor):
        return jnp.transpose(factor, (0, 1, 3, 4, 2, 5)).reshape(
            rows * total // 2, 2, rows, size, size
        )

    lower, upper = blocks(lower_factor_t), blocks(upper_factor_t)
    own = local_call(turn_kernel, "turn", (rows, width, size), bf16, [rhs])

    def level(factor, direction, count):
        first, base = (0, 0) if count == 2 else (2, 2 * total)
        kernel = functools.partial(
            pack_level_kernel, direction, base, count, first, count * total
        )
        return lambda table: pack_call(
            kernel, "pack_level", (count * half, size, size), 2 * count, factor, table
        )

    def pack_down(table):
        return pack_call(
            pack_down_kernel, "pack_down", (total, size, size), 2, lower, table, upper_snode, parent, pattern
        )

    def pack_up(table):
        return pack_call(
            pack_up_kernel, "pack_up", (2, total // 2, size, size), 4, upper, table, upper_snode, parent, pattern
        )

    def halves(kernels, name, count, width_in, block, direction, table, pack):
        pieces, mine, theirs = gather(block, direction, table, pack)
        shape = (count, width, size)
        sent = local_call(kernels[1], name + "_other", shape, f32, [*pieces, theirs], width_in)
        brought = swap(sent, 1)
        kept = local_call(kernels[0], name, shape, f32, [*pieces, mine], width_in)
        return kept, brought

    def window(name, count, block, direction, table, factor):
        kernels = [functools.partial(window_kernel, direction, flip) for flip in (0, 1)]
        return halves(
            kernels, name, count, half * size, block, direction, table, level(factor, direction, count)
        )

    kept, brought = window("forward_lower", 2, own[:2], 1, lower_snode, lower)
    forward_lower = kept + brought
    known = forward_lower.astype(bf16)
    kept, brought = halves(
        [down_kernel] * 2, "coupling", 1, total * size, known, 0, lower_snode, pack_down
    )
    coupling = (kept + brought).astype(bf16).astype(f32)
    difference = (own[2:].astype(f32) - coupling).astype(bf16)
    kept, brought = window("forward_upper", 1, difference, 1, upper_snode, lower)
    forward_upper = kept + brought
    kept, brought = window("backward_upper", 1, forward_upper.astype(bf16), -1, upper_snode, upper)
    backward_upper = kept + brought
    forward_solution = local_call(
        forward_out_kernel,
        "forward_out",
        (rows, 1, size, width),
        f32,
        [forward_lower, forward_upper],
    )
    kept, brought = halves(
        [up_kernel] * 2,
        "correction",
        2,
        total // 2 * size,
        backward_upper.astype(bf16),
        0,
        lower_snode,
        pack_up,
    )
    correction = (kept + brought).astype(bf16).astype(f32)
    remainder = (known.astype(f32) - correction).astype(bf16)
    kept, brought = window("backward_lower", 2, remainder, -1, lower_snode, upper)
    backward_solution = local_call(
        backward_out_kernel,
        "backward_out",
        (rows, 1, size, width),
        f32,
        [kept, brought, backward_upper],
    )
    return forward_solution, backward_solution


def block_masks(lower_snode, upper_snode, parent, pattern):
    count_lower = parent.shape[0]
    snode_ids = jnp.concatenate([lower_snode, upper_snode + count_lower])
    same = snode_ids[:, None] == snode_ids[None, :]
    onehot = (lower_snode[:, None] == jnp.arange(count_lower, dtype=jnp.int32)[None, :]).astype(
        jnp.int32
    )
    parent_block = jnp.sum(onehot * parent[:, 0][None, :], axis=1)
    pattern_block = jnp.sum(pattern[:, None, :] * onehot[None, :, :], axis=2)
    link = (upper_snode[:, None] == parent_block[None, :]) & (pattern_block == 1)
    return (same, link)


def couplings(link):
    upper_count, lower_count = link.shape
    total = upper_count + lower_count
    couple_lower = jnp.concatenate(
        [
            jnp.zeros((lower_count, total), bool),
            jnp.concatenate([link, jnp.zeros((upper_count, upper_count), bool)], 1),
        ],
        0,
    )
    couple_upper = jnp.concatenate(
        [
            jnp.concatenate([jnp.zeros((lower_count, lower_count), bool), link.T], 1),
            jnp.zeros((upper_count, total), bool),
        ],
        0,
    )
    return (couple_lower, couple_upper)


def on_device(rhs, lower_factor_t, upper_factor_t, lower_snode, upper_snode, parent, pattern):
    rows_axis = lax.axis_size("prow")
    row_index = lax.axis_index("prow")
    col_index = lax.axis_index("pcol")
    blocks_local = rhs.shape[0]
    sub_rows = rhs.shape[2]
    col_group = lower_factor_t.shape[1]
    block_size = lower_factor_t.shape[2]
    lower_local = lower_snode.shape[0] // rows_axis
    same, link = block_masks(lower_snode, upper_snode, parent, pattern)
    couple_lower, couple_upper = couplings(link)
    all_blocks = same.shape[0]

    def local_blocks(whole):
        selected = lax.dynamic_index_in_dim(
            whole.reshape(blocks_local, rows_axis, all_blocks), row_index, 1, keepdims=False
        )
        selected = selected.reshape(blocks_local, blocks_local, rows_axis)
        selected = lax.dynamic_slice_in_dim(selected, col_index * col_group, col_group, 2)
        return jnp.transpose(selected, (1, 2, 0)).reshape(
            blocks_local, col_group, 1, blocks_local, 1, 1
        )

    local_ids = jnp.arange(blocks_local, dtype=jnp.int32)
    row_elem = (
        (local_ids[:, None] * rows_axis + row_index) * block_size
        + jnp.arange(block_size, dtype=jnp.int32)[None, :]
    ).reshape(1, 1, 1, blocks_local, 1, block_size)
    own_cols = col_index * col_group + jnp.arange(col_group, dtype=jnp.int32)
    col_block = local_ids[:, None] * rows_axis + own_cols[None, :]
    col_elem = (
        col_block[:, :, None] * block_size + jnp.arange(block_size, dtype=jnp.int32)[None, None, :]
    ).reshape(blocks_local, col_group, block_size, 1, 1, 1)
    same_local = local_blocks(same)
    keep_lower = same_local & (row_elem >= col_elem) | local_blocks(couple_lower)
    keep_upper = same_local & (row_elem <= col_elem) | local_blocks(couple_upper)
    lower_kept = jnp.where(keep_lower, lower_factor_t, jnp.zeros((), lower_factor_t.dtype))
    upper_kept = jnp.where(keep_upper, upper_factor_t, jnp.zeros((), upper_factor_t.dtype))

    def apply_factor(factor, vector, col_range, row_range):
        window = factor[col_range[0] : col_range[1], :, :, row_range[0] : row_range[1], 0, :]
        pieces_in = lax.all_gather(vector, "prow", axis=1, tiled=True)
        selector = (
            jnp.arange(pieces_in.shape[1], dtype=jnp.int32)[:, None] == own_cols[None, :]
        ).astype(jnp.bfloat16)
        picked = jnp.einsum(
            "rjen,jq->rqen", pieces_in, selector, preferred_element_type=jnp.float32
        ).astype(jnp.bfloat16)
        summed = lax.dot_general(
            window, picked, (((0, 1, 2), (0, 1, 2)), ((), ())), preferred_element_type=jnp.float32
        )[:, None]
        return lax.psum(summed, "pcol")

    source = lax.all_gather(rhs, "pcol", axis=2, tiled=True)
    rhs_width = source.shape[3]
    lower_span = (0, lower_local)
    upper_span = (lower_local, blocks_local)
    rhs_lower = source[:lower_local]
    rhs_upper = source[lower_local:]
    forward_lower = apply_factor(lower_kept, rhs_lower, lower_span, lower_span)
    lower_known = forward_lower.astype(jnp.bfloat16)
    coupling = apply_factor(lower_kept, lower_known, lower_span, upper_span).astype(jnp.bfloat16)
    joined = apply_factor(
        lower_kept, jnp.concatenate([rhs_upper, coupling], 3), upper_span, upper_span
    )
    upper_direct = joined[..., :rhs_width]
    upper_update = joined[..., rhs_width:]
    forward_upper = upper_direct - upper_update
    upper_known = forward_upper.astype(jnp.bfloat16)
    backward_upper = apply_factor(upper_kept, upper_known, upper_span, upper_span)
    back_known = backward_upper.astype(jnp.bfloat16)
    correction = apply_factor(upper_kept, back_known, upper_span, lower_span).astype(jnp.bfloat16)
    joined_lower = apply_factor(
        upper_kept, jnp.concatenate([lower_known, correction], 3), lower_span, lower_span
    )
    lower_direct = joined_lower[..., :rhs_width]
    lower_update = joined_lower[..., rhs_width:]
    backward_lower = lower_direct - lower_update
    forward_solution = jnp.concatenate([forward_lower, forward_upper], 0)
    backward_solution = jnp.concatenate([backward_lower, backward_upper], 0)
    forward_solution = lax.dynamic_slice_in_dim(forward_solution, col_index * sub_rows, sub_rows, 2)
    backward_solution = lax.dynamic_slice_in_dim(
        backward_solution, col_index * sub_rows, sub_rows, 2
    )
    return (forward_solution, backward_solution)


def solution(mesh):
    placed = (
        P("parts", "prow", "pcol", None),
        P("parts", "pcol", None, None, "prow", None),
        P("parts", "pcol", None, None, "prow", None),
        P("parts"),
        P("parts"),
        P("parts", None),
        P("parts", None),
    )
    total = PLANE * PLANES
    simple = mesh.shape["prow"] == total and mesh.shape["pcol"] == 1
    return jax.shard_map(
        fast_device if simple else on_device,
        mesh=mesh,
        in_specs=placed,
        out_specs=(P("parts", "prow", "pcol", None), P("parts", "prow", "pcol", None)),
        check_vma=False,
    )
```

```python
import functools
import jax
import jax.numpy as jnp
from jax import lax
from jax.experimental import pallas as pl
from jax.experimental.pallas import tpu as pltpu
from jax.sharding import PartitionSpec as P

SPAN = 16
PLANE = 8
PLANES = 4
VMEM_BYTES = 48 * 1024 * 1024


def window_start(block, direction, count):
    if direction > 0:
        return jnp.maximum(block - (SPAN - 1), 0)
    return jnp.minimum(block, count - SPAN)


def keep_window(out, block, start, direction, snode, first):
    own = snode[block]

    def clear(step, carry):
        other = start + step
        if direction > 0:
            kept = (snode[other] == own) & (other <= block)
        else:
            kept = (snode[other] == own) & (other >= block)

        @pl.when(jnp.logical_not(kept))
        def _():
            out[first + step] = jnp.zeros(out.shape[1:], out.dtype)

        return carry

    lax.fori_loop(0, SPAN, clear, 0)
    size = out.shape[1]
    col = lax.broadcasted_iota(jnp.int32, (size, size), 0)
    row = lax.broadcasted_iota(jnp.int32, (size, size), 1)
    tri = row >= col if direction > 0 else row <= col
    diagonal = out[first + block - start]
    out[first + block - start] = jnp.where(tri, diagonal, jnp.zeros_like(diagonal))


def pack_level_kernel(direction, base, rows, row_first, count, factor, snode, out, sems):
    me = lax.axis_index("prow")
    copies = []
    for row in range(rows):
        block = row * PLANE * PLANES + me
        start = window_start(block, direction, count)
        copy = pltpu.make_async_copy(
            factor.at[pl.ds(base + start, SPAN), row_first + row],
            out.at[pl.ds(row * SPAN, SPAN)],
            sems.at[row],
        )
        copy.start()
        copies.append((copy, block, start))
    for row, (copy, block, start) in enumerate(copies):
        copy.wait()
        keep_window(out, block, start, direction, snode, row * SPAN)


def pack_level(factor, snode, direction, base, rows, row_first, count):
    size = factor.shape[-1]
    return pl.pallas_call(
        functools.partial(pack_level_kernel, direction, base, rows, row_first, count),
        out_shape=jax.ShapeDtypeStruct((rows * SPAN, size, size), factor.dtype),
        in_specs=[
            pl.BlockSpec(memory_space=pl.ANY),
            pl.BlockSpec(memory_space=pltpu.SMEM),
        ],
        out_specs=pl.BlockSpec(memory_space=pltpu.VMEM),
        scratch_shapes=[pltpu.SemaphoreType.DMA((rows,))],
        compiler_params=pltpu.CompilerParams(vmem_limit_bytes=VMEM_BYTES),
        cost_estimate=pl.CostEstimate(flops=0, bytes_accessed=4 * rows * SPAN * size * size, transcendentals=0),
        name="pack_level",
    )(factor, snode)


def pack_down_kernel(factor, lower_snode, upper_snode, parent, pattern, out, sem):
    me = lax.axis_index("prow")
    count = out.shape[0]
    copy = pltpu.make_async_copy(factor.at[pl.ds(0, count), 2], out, sem)
    copy.start()
    copy.wait()

    def clear(block, carry):
        child = lower_snode[block]
        linked = (parent[child, 0] == upper_snode[me]) & (pattern[me, child] == 1)

        @pl.when(jnp.logical_not(linked))
        def _():
            out[block] = jnp.zeros(out.shape[1:], out.dtype)

        return carry

    lax.fori_loop(0, count, clear, 0)


def pack_up_kernel(factor, lower_snode, upper_snode, parent, pattern, out, sems):
    me = lax.axis_index("prow")
    count = out.shape[1]
    copies = []
    for row in range(2):
        copy = pltpu.make_async_copy(
            factor.at[pl.ds(2 * count, count), row], out.at[row], sems.at[row]
        )
        copy.start()
        copies.append(copy)
    for row in range(2):
        copies[row].wait()
        child = lower_snode[row * count + me]
        above = parent[child, 0]

        def clear(block, carry):
            linked = (above == upper_snode[block]) & (pattern[block, child] == 1)

            @pl.when(jnp.logical_not(linked))
            def _():
                out[row, block] = jnp.zeros(out.shape[2:], out.dtype)

            return carry

        lax.fori_loop(0, count, clear, 0)


def pack_coupling(kernel, name, shape, sems, factor, *tables):
    return pl.pallas_call(
        kernel,
        out_shape=jax.ShapeDtypeStruct(shape, factor.dtype),
        in_specs=[pl.BlockSpec(memory_space=pl.ANY)]
        + [pl.BlockSpec(memory_space=pltpu.SMEM)] * 4,
        out_specs=pl.BlockSpec(memory_space=pltpu.VMEM),
        scratch_shapes=[sems],
        compiler_params=pltpu.CompilerParams(vmem_limit_bytes=VMEM_BYTES),
        cost_estimate=pl.CostEstimate(flops=0, bytes_accessed=4 * 64 * 128 * 128, transcendentals=0),
        name=name,
    )(factor, *tables)


def gather(block, direction, table, pack):
    total = PLANE * PLANES

    def swap(value, distance):
        return lax.ppermute(value, "prow", [(i, i ^ distance) for i in range(total)])

    parts = [block[None]]
    if direction == 0:
        parts += [swap(block[None], PLANE * step) for step in range(1, PLANES)]
    else:
        for step in (1, 2):
            pairs = [(i, (i + direction * step * PLANE) % total) for i in range(total)]
            parts.append(lax.ppermute(block[None], "prow", pairs))
    packed = pack(lax.optimization_barrier((table, block))[0])
    parts, packed = lax.optimization_barrier((parts, packed))
    stacked = jnp.concatenate(parts, 0)
    pieces = {0: stacked}
    if direction == 0:
        sent = {1: stacked, 2: stacked, 4: stacked}
    else:
        near, far = jnp.concatenate(parts[:2], 0), jnp.concatenate(parts[1:], 0)
        me = lax.axis_index("prow")
        sent = {}
        for bit in (1, 2, 4):
            after = (me & bit) != 0
            sent[bit] = jnp.where(after if direction > 0 else jnp.logical_not(after), far, near)
    for k in (6, 2, 4):
        pieces[k] = swap(sent[2 if k == 2 else 4], k)
    pieces[1] = swap(sent[1], 1)
    for k in (6, 2, 4):
        pieces[k + 1] = swap(pieces[k], 1)
    return [pieces[k] for k in range(PLANE)], packed


def copy_window(pieces, xs, block, start, direction):
    me = lax.axis_index("prow")
    offset = me & (PLANE - 1)
    size = xs.shape[0]
    for k in range(PLANE):
        other = offset ^ k
        first = (other - start) & (PLANE - 1)
        skipped = jnp.int32(0)
        if k > 0:
            skipped = (other > offset if direction > 0 else other < offset).astype(jnp.int32)
        for half in range(SPAN // PLANE):
            slot = first + half * PLANE
            source = start + slot
            apart = direction * (block // PLANE - source // PLANE)
            apart = jnp.clip(apart - skipped, 0, pieces[k].shape[0] - 1)
            level = source // (PLANE * PLANES) if pieces[k].shape[1] > 1 else 0
            at = pl.multiple_of(slot * size, size)
            xs[:, pl.ds(at, size)] = pieces[k][apart, level]


def dot(left, right):
    return jnp.dot(left, right, preferred_element_type=jnp.float32)


def forward_lower_kernel(*refs):
    pieces, (factor, solved, known, xs) = refs[:PLANE], refs[PLANE:]
    me = lax.axis_index("prow")
    size = xs.shape[0]
    for row in range(2):
        block = row * PLANE * PLANES + me
        start = window_start(block, 1, 2 * PLANE * PLANES)
        copy_window(pieces, xs, block, start, 1)
        result = dot(xs[...], factor[row * SPAN : (row + 1) * SPAN].reshape(SPAN * size, size))
        solved[row] = result
        known[row] = result.astype(known.dtype)


def coupling_kernel(*refs):
    pieces, (factor, rhs, out, xs) = refs[:PLANE], refs[PLANE:]
    me = lax.axis_index("prow")
    offset, plane = me & (PLANE - 1), me // PLANE
    size = xs.shape[0]
    for k in range(PLANE):
        for along in range(PLANES):
            for row in range(2):
                source = row * PLANE * PLANES + (plane ^ along) * PLANE + (offset ^ k)
                xs[:, pl.ds(pl.multiple_of(source * size, size), size)] = pieces[k][along, row]
    result = dot(xs[...], factor[...].reshape(2 * PLANE * PLANES * size, size))
    rounded = result.astype(out.dtype).astype(jnp.float32)
    out[0] = (rhs[2].astype(jnp.float32) - rounded).astype(out.dtype)


def upper_kernel(direction, *refs):
    pieces, (factor, solved, known, xs) = refs[:PLANE], refs[PLANE:]
    me = lax.axis_index("prow")
    size = xs.shape[0]
    start = window_start(me, direction, PLANE * PLANES)
    copy_window(pieces, xs, me, start, direction)
    result = dot(xs[...], factor[...].reshape(SPAN * size, size))
    solved[0] = result
    known[0] = result.astype(known.dtype)


def correction_kernel(*refs):
    pieces, (factor, solved, out, xs) = refs[:PLANE], refs[PLANE:]
    me = lax.axis_index("prow")
    offset, plane = me & (PLANE - 1), me // PLANE
    size = xs.shape[0]
    for k in range(PLANE):
        for along in range(PLANES):
            source = (plane ^ along) * PLANE + (offset ^ k)
            xs[:, pl.ds(pl.multiple_of(source * size, size), size)] = pieces[k][along, 0]
    for row in range(2):
        result = dot(xs[...], factor[row].reshape(PLANE * PLANES * size, size))
        known = solved[row].astype(out.dtype).astype(jnp.float32)
        rounded = result.astype(out.dtype).astype(jnp.float32)
        out[row] = (known - rounded).astype(out.dtype)


def backward_lower_kernel(*refs):
    pieces, (factor, upper, out, xs) = refs[:PLANE], refs[PLANE:]
    me = lax.axis_index("prow")
    size = xs.shape[0]
    for row in range(2):
        block = row * PLANE * PLANES + me
        start = window_start(block, -1, 2 * PLANE * PLANES)
        copy_window(pieces, xs, block, start, -1)
        result = dot(xs[...], factor[row * SPAN : (row + 1) * SPAN].reshape(SPAN * size, size))
        out[row, 0] = result.T
    out[2, 0] = upper[0].T


def turn_kernel(value, out):
    for row in range(3):
        out[row] = value[row, 0].astype(jnp.float32).T.astype(out.dtype)


def forward_out_kernel(lower, upper, out):
    for row in range(2):
        out[row, 0] = lower[row].T
    out[2, 0] = upper[0].T


def local_call(kernel, name, shapes, operands, width=0, flops=0):
    size = 128
    scratch = [pltpu.VMEM((size, width), jnp.bfloat16)] if width else []
    outs = [jax.ShapeDtypeStruct(*shape) for shape in shapes]
    return pl.pallas_call(
        kernel,
        out_shape=outs,
        in_specs=[pl.BlockSpec(memory_space=pltpu.VMEM)] * len(operands),
        out_specs=[pl.BlockSpec(memory_space=pltpu.VMEM)] * len(outs),
        scratch_shapes=scratch,
        compiler_params=pltpu.CompilerParams(vmem_limit_bytes=VMEM_BYTES),
        cost_estimate=pl.CostEstimate(flops=flops, bytes_accessed=1 << 20, transcendentals=0),
        name=name,
    )(*operands)


def fast_device(rhs, lower_factor_t, upper_factor_t, lower_snode, upper_snode, parent, pattern):
    rows, _, size, width = rhs.shape
    total = PLANE * PLANES
    f32, bf16 = jnp.float32, jnp.bfloat16

    def blocks(factor):
        return jnp.transpose(factor, (0, 1, 3, 4, 2, 5)).reshape(rows * total, rows, size, size)

    lower, upper = blocks(lower_factor_t), blocks(upper_factor_t)
    tables = (lower_snode, upper_snode, parent, pattern)
    own = local_call(turn_kernel, "turn", [((rows, width, size), bf16)], [rhs])[0]

    forward, backward, whole = 1, -1, 0

    def pack_l1(table):
        return pack_level(lower, table, 1, 0, 2, 0, 2 * total)

    def pack_c(table):
        return pack_coupling(
            pack_down_kernel,
            "pack_down",
            (2 * total, size, size),
            pltpu.SemaphoreType.DMA,
            lower,
            table,
            *tables[1:],
        )

    def pack_l2(table):
        return pack_level(lower, table, 1, 2 * total, 1, 2, total)

    def pack_u2(table):
        return pack_level(upper, table, -1, 2 * total, 1, 2, total)

    def pack_k(table):
        return pack_coupling(
            pack_up_kernel,
            "pack_up",
            (2, total, size, size),
            pltpu.SemaphoreType.DMA((2,)),
            upper,
            table,
            *tables[1:],
        )

    def pack_u1(table):
        return pack_level(upper, table, -1, 0, 2, 0, 2 * total)

    pieces, packed = gather(own[:2], forward, lower_snode, pack_l1)
    solved, known = local_call(
        forward_lower_kernel,
        "forward_lower",
        [((2, width, size), f32), ((2, width, size), bf16)],
        [*pieces, packed],
        SPAN * size,
    )
    pieces, packed = gather(known, whole, lower_snode, pack_c)
    (difference,) = local_call(
        coupling_kernel,
        "coupling",
        [((1, width, size), bf16)],
        [*pieces, packed, own],
        2 * total * size,
    )
    pieces, packed = gather(difference, forward, upper_snode, pack_l2)
    forward_upper, upper_known = local_call(
        functools.partial(upper_kernel, 1),
        "forward_upper",
        [((1, width, size), f32), ((1, width, size), bf16)],
        [*pieces, packed],
        SPAN * size,
    )
    pieces, packed = gather(upper_known, backward, upper_snode, pack_u2)
    (forward_solution,) = local_call(
        forward_out_kernel,
        "forward_out",
        [((rows, 1, size, width), f32)],
        [solved, forward_upper],
    )
    backward_upper, back_known = local_call(
        functools.partial(upper_kernel, -1),
        "backward_upper",
        [((1, width, size), f32), ((1, width, size), bf16)],
        [*pieces, packed],
        SPAN * size,
    )
    pieces, packed = gather(back_known, whole, lower_snode, pack_k)
    (remainder,) = local_call(
        correction_kernel,
        "correction",
        [((2, width, size), bf16)],
        [*pieces, packed, solved],
        total * size,
    )
    pieces, packed = gather(remainder, backward, lower_snode, pack_u1)
    (backward_solution,) = local_call(
        backward_lower_kernel,
        "backward_lower",
        [((rows, 1, size, width), f32)],
        [*pieces, packed, backward_upper],
        SPAN * size,
    )
    return forward_solution, backward_solution


def block_masks(lower_snode, upper_snode, parent, pattern):
    count_lower = parent.shape[0]
    snode_ids = jnp.concatenate([lower_snode, upper_snode + count_lower])
    same = snode_ids[:, None] == snode_ids[None, :]
    onehot = (lower_snode[:, None] == jnp.arange(count_lower, dtype=jnp.int32)[None, :]).astype(
        jnp.int32
    )
    parent_block = jnp.sum(onehot * parent[:, 0][None, :], axis=1)
    pattern_block = jnp.sum(pattern[:, None, :] * onehot[None, :, :], axis=2)
    link = (upper_snode[:, None] == parent_block[None, :]) & (pattern_block == 1)
    return (same, link)


def couplings(link):
    upper_count, lower_count = link.shape
    total = upper_count + lower_count
    couple_lower = jnp.concatenate(
        [
            jnp.zeros((lower_count, total), bool),
            jnp.concatenate([link, jnp.zeros((upper_count, upper_count), bool)], 1),
        ],
        0,
    )
    couple_upper = jnp.concatenate(
        [
            jnp.concatenate([jnp.zeros((lower_count, lower_count), bool), link.T], 1),
            jnp.zeros((upper_count, total), bool),
        ],
        0,
    )
    return (couple_lower, couple_upper)


def on_device(rhs, lower_factor_t, upper_factor_t, lower_snode, upper_snode, parent, pattern):
    rows_axis = lax.axis_size("prow")
    row_index = lax.axis_index("prow")
    col_index = lax.axis_index("pcol")
    blocks_local = rhs.shape[0]
    sub_rows = rhs.shape[2]
    col_group = lower_factor_t.shape[1]
    block_size = lower_factor_t.shape[2]
    lower_local = lower_snode.shape[0] // rows_axis
    same, link = block_masks(lower_snode, upper_snode, parent, pattern)
    couple_lower, couple_upper = couplings(link)
    all_blocks = same.shape[0]

    def local_blocks(whole):
        selected = lax.dynamic_index_in_dim(
            whole.reshape(blocks_local, rows_axis, all_blocks), row_index, 1, keepdims=False
        )
        selected = selected.reshape(blocks_local, blocks_local, rows_axis)
        selected = lax.dynamic_slice_in_dim(selected, col_index * col_group, col_group, 2)
        return jnp.transpose(selected, (1, 2, 0)).reshape(
            blocks_local, col_group, 1, blocks_local, 1, 1
        )

    local_ids = jnp.arange(blocks_local, dtype=jnp.int32)
    row_elem = (
        (local_ids[:, None] * rows_axis + row_index) * block_size
        + jnp.arange(block_size, dtype=jnp.int32)[None, :]
    ).reshape(1, 1, 1, blocks_local, 1, block_size)
    own_cols = col_index * col_group + jnp.arange(col_group, dtype=jnp.int32)
    col_block = local_ids[:, None] * rows_axis + own_cols[None, :]
    col_elem = (
        col_block[:, :, None] * block_size + jnp.arange(block_size, dtype=jnp.int32)[None, None, :]
    ).reshape(blocks_local, col_group, block_size, 1, 1, 1)
    same_local = local_blocks(same)
    keep_lower = same_local & (row_elem >= col_elem) | local_blocks(couple_lower)
    keep_upper = same_local & (row_elem <= col_elem) | local_blocks(couple_upper)
    lower_kept = jnp.where(keep_lower, lower_factor_t, jnp.zeros((), lower_factor_t.dtype))
    upper_kept = jnp.where(keep_upper, upper_factor_t, jnp.zeros((), upper_factor_t.dtype))

    def apply_factor(factor, vector, col_range, row_range):
        window = factor[col_range[0] : col_range[1], :, :, row_range[0] : row_range[1], 0, :]
        pieces_in = lax.all_gather(vector, "prow", axis=1, tiled=True)
        selector = (
            jnp.arange(pieces_in.shape[1], dtype=jnp.int32)[:, None] == own_cols[None, :]
        ).astype(jnp.bfloat16)
        picked = jnp.einsum(
            "rjen,jq->rqen", pieces_in, selector, preferred_element_type=jnp.float32
        ).astype(jnp.bfloat16)
        summed = lax.dot_general(
            window, picked, (((0, 1, 2), (0, 1, 2)), ((), ())), preferred_element_type=jnp.float32
        )[:, None]
        return lax.psum(summed, "pcol")

    source = lax.all_gather(rhs, "pcol", axis=2, tiled=True)
    rhs_width = source.shape[3]
    lower_span = (0, lower_local)
    upper_span = (lower_local, blocks_local)
    rhs_lower = source[:lower_local]
    rhs_upper = source[lower_local:]
    forward_lower = apply_factor(lower_kept, rhs_lower, lower_span, lower_span)
    lower_known = forward_lower.astype(jnp.bfloat16)
    coupling = apply_factor(lower_kept, lower_known, lower_span, upper_span).astype(jnp.bfloat16)
    joined = apply_factor(
        lower_kept, jnp.concatenate([rhs_upper, coupling], 3), upper_span, upper_span
    )
    upper_direct = joined[..., :rhs_width]
    upper_update = joined[..., rhs_width:]
    forward_upper = upper_direct - upper_update
    upper_known = forward_upper.astype(jnp.bfloat16)
    backward_upper = apply_factor(upper_kept, upper_known, upper_span, upper_span)
    back_known = backward_upper.astype(jnp.bfloat16)
    correction = apply_factor(upper_kept, back_known, upper_span, lower_span).astype(jnp.bfloat16)
    joined_lower = apply_factor(
        upper_kept, jnp.concatenate([lower_known, correction], 3), lower_span, lower_span
    )
    lower_direct = joined_lower[..., :rhs_width]
    lower_update = joined_lower[..., rhs_width:]
    backward_lower = lower_direct - lower_update
    forward_solution = jnp.concatenate([forward_lower, forward_upper], 0)
    backward_solution = jnp.concatenate([backward_lower, backward_upper], 0)
    forward_solution = lax.dynamic_slice_in_dim(forward_solution, col_index * sub_rows, sub_rows, 2)
    backward_solution = lax.dynamic_slice_in_dim(
        backward_solution, col_index * sub_rows, sub_rows, 2
    )
    return (forward_solution, backward_solution)


def solution(mesh):
    placed = (
        P("parts", "prow", "pcol", None),
        P("parts", "pcol", None, None, "prow", None),
        P("parts", "pcol", None, None, "prow", None),
        P("parts"),
        P("parts"),
        P("parts", None),
        P("parts", None),
    )
    total = PLANE * PLANES
    simple = mesh.shape["prow"] == total and mesh.shape["pcol"] == 1
    return jax.shard_map(
        fast_device if simple else on_device,
        mesh=mesh,
        in_specs=placed,
        out_specs=(P("parts", "prow", "pcol", None), P("parts", "prow", "pcol", None)),
        check_vma=False,
    )
```

```python
import functools
import jax
import jax.numpy as jnp
from jax import lax
from jax.experimental import pallas as pl
from jax.experimental.pallas import tpu as pltpu
from jax.sharding import PartitionSpec as P

SPAN = 16
PLANE = 8
PLANES = 4
VMEM_BYTES = 48 * 1024 * 1024


def window_start(block, direction, count):
    if direction > 0:
        return jnp.maximum(block - (SPAN - 1), 0)
    return jnp.minimum(block, count - SPAN)


def first_pair(start, parity):
    return (start + 1 - parity) // 2


def start_window(direction, base, rows, row_first, count, factor, out, sems):
    me = lax.axis_index("prow")
    half = SPAN // 2
    copies = []
    for row in range(rows):
        block = row * PLANE * PLANES + me
        start = window_start(block, direction, count)
        for side in range(2):
            parity = (me & 1) ^ side
            pair = first_pair(start, parity)
            at = row * SPAN + side * half
            copy = pltpu.make_async_copy(
                factor.at[pl.ds(base // 2 + pair, half), parity, row_first + row],
                out.at[pl.ds(at, half)],
                sems.at[2 * row + side],
            )
            copy.start()
            copies.append((copy, block, pair, side, at))
    return copies


def keep_window(direction, copies, snode, out):
    me = lax.axis_index("prow")
    half, size = SPAN // 2, out.shape[1]
    col = lax.broadcasted_iota(jnp.int32, (size, size), 0)
    line = lax.broadcasted_iota(jnp.int32, (size, size), 1)
    tri = line >= col if direction > 0 else line <= col
    zero = jnp.zeros((size, size), out.dtype)
    for copy, block, pair, side, at in copies:
        copy.wait()
        own = snode[block]
        for step in range(half):
            column = 2 * (pair + step) + ((me & 1) ^ side)
            kept = snode[column] == own
            kept = kept & (column <= block if direction > 0 else column >= block)
            out[at + step] = jnp.where(kept, out[at + step], zero)
        if side == 0:
            diagonal = at + block // 2 - pair
            out[diagonal] = jnp.where(tri, out[diagonal], zero)


def pack_level_kernel(direction, base, rows, row_first, count, factor, after, rules, out, sems):
    copies = start_window(direction, base, rows, row_first, count, factor, out, sems)
    keep_window(direction, copies, rules.at[0 if rows == 2 else 1], out)


def pack_up_kernel(factor, after, rules, out, sems):
    me = lax.axis_index("prow")
    total = PLANE * PLANES
    many, size = total // 2, out.shape[1]
    copies = []
    for row in range(2):
        for side in range(2):
            at = (2 * row + side) * many
            copy = pltpu.make_async_copy(
                factor.at[pl.ds(total, many), (me & 1) ^ side, row],
                out.at[pl.ds(at, many)],
                sems.at[2 * row + side],
            )
            copy.start()
            copies.append((copy, row, side, at))
    zero = jnp.zeros((size, size), out.dtype)
    for copy, row, side, at in copies:
        child = rules[0, row * total + me]
        above = rules[2, child]
        copy.wait()
        for pair in range(many):
            block = 2 * pair + ((me & 1) ^ side)
            linked = (above == rules[1, block]) & (rules[3 + child, block] == 1)
            out[at + pair] = jnp.where(linked, out[at + pair], zero)


def pack_call(kernel, name, blocks, copies, factor, after, rules):
    size, dtype = factor.shape[-1], factor.dtype
    return pl.pallas_call(
        kernel,
        out_shape=jax.ShapeDtypeStruct((blocks, size, size), dtype),
        in_specs=[pl.BlockSpec(memory_space=pl.ANY)] * 2
        + [pl.BlockSpec(memory_space=pltpu.SMEM)],
        out_specs=pl.BlockSpec(memory_space=pltpu.VMEM),
        scratch_shapes=[pltpu.SemaphoreType.DMA((copies,))],
        compiler_params=pltpu.CompilerParams(vmem_limit_bytes=VMEM_BYTES),
        cost_estimate=pl.CostEstimate(
            flops=0, bytes_accessed=2 * blocks * size * size * dtype.itemsize, transcendentals=0
        ),
        name=name,
    )(factor, after, rules)


def first_pack_kernel(
    factor, after, rules, mine, even, odd, table, kids, sems
):
    me = lax.axis_index("prow")
    offset, plane = me & (PLANE - 1), me // PLANE
    total = PLANE * PLANES
    count, children = 2 * total, rules.shape[0] - 3
    lower_snode, upper_snode, parent = rules.at[0], rules.at[1], rules.at[2]
    size = mine.shape[1]
    windows = start_window(1, 0, 2, 0, count, factor, mine, sems)
    begins = []
    for child in range(children):
        found = jnp.int32(0)
        for bit in reversed(range(count.bit_length() - 1)):
            ahead = found + (1 << bit)
            found = jnp.where(lower_snode[ahead - 1] < child, ahead, found)
        begins.append(found)
    parents = [parent[child] for child in range(children)]

    def children_of(above):
        first, first_at = jnp.int32(0), jnp.int32(0)
        last, last_at = jnp.int32(0), jnp.int32(0)
        for child in range(children):
            match = parents[child] == above
            last, last_at = jnp.where(match, child, last), jnp.where(match, begins[child], last_at)
        for child in reversed(range(children)):
            match = parents[child] == above
            first, first_at = jnp.where(match, child, first), jnp.where(match, begins[child], first_at)
        return (first, first_at), (last, last_at)

    def column(start, place, step):
        return start + ((place - start) & (PLANE - 1)) + step * PLANE

    low, high = children_of(upper_snode[me])
    copies = []
    for side, (child, start) in enumerate((low, high)):
        at = jnp.minimum(start, count - SPAN - 2)
        copy = pltpu.make_async_copy(
            factor.at[pl.ds(at // 2, SPAN // 2 + 1), :, 2], kids.at[side], sems.at[4 + side]
        )
        copy.start()
        linked = rules[3 + child, me] == 1
        if side:
            linked = linked & (low[0] != high[0])
        copies.append((copy, child, start, at, linked))
    for k in range(PLANE):
        pair = children_of(upper_snode[plane * PLANE + (offset ^ k)])
        for slot in range(4):
            found = column(pair[slot // 2][1], offset, slot % 2)
            table[4 * k + slot] = jnp.minimum(found, count - 1)
    keep_window(1, windows, lower_snode, mine)
    zero = jnp.zeros((size, size), mine.dtype)
    for side, (copy, child, start, at, linked) in enumerate(copies):
        copy.wait()
        for k in range(PLANE):
            for step in range(2):
                found = column(start, offset ^ k, step)
                source = jnp.minimum(found, count - 1)
                kept = linked & (found < count) & (lower_snode[source] == child)
                out = odd if k % 2 else even
                near = jnp.minimum(source // 2 - at // 2, SPAN // 2)
                value = kids[side, near, source % 2]
                out[4 * (k // 2) + 2 * side + step] = jnp.where(kept, value, zero)


def first_pack(factor, after, rules):
    size, dtype = factor.shape[-1], factor.dtype
    counts = (2 * SPAN, SPAN, SPAN)
    vmem, smem = (pl.BlockSpec(memory_space=space) for space in (pltpu.VMEM, pltpu.SMEM))
    return pl.pallas_call(
        first_pack_kernel,
        out_shape=[jax.ShapeDtypeStruct((count, size, size), dtype) for count in counts]
        + [jax.ShapeDtypeStruct((4 * PLANE,), jnp.int32)],
        in_specs=[pl.BlockSpec(memory_space=pl.ANY)] * 2 + [smem],
        out_specs=[vmem] * 3 + [smem],
        scratch_shapes=[
            pltpu.VMEM((2, SPAN // 2 + 1, 2, size, size), dtype),
            pltpu.SemaphoreType.DMA((6,)),
        ],
        compiler_params=pltpu.CompilerParams(vmem_limit_bytes=VMEM_BYTES),
        cost_estimate=pl.CostEstimate(
            flops=0, bytes_accessed=2 * sum(counts) * size * size * dtype.itemsize, transcendentals=0
        ),
        name="first_pack",
    )(factor, after, rules)


def swap(value, distance):
    return lax.ppermute(value, "prow", [(i, i ^ distance) for i in range(PLANE * PLANES)])


def along_z(block, direction):
    total = PLANE * PLANES
    parts = [block[None]]
    if direction == 0:
        return parts + [swap(block[None], PLANE * step) for step in range(1, PLANES)]
    for step in (1, 2):
        pairs = [(i, (i + direction * step * PLANE) % total) for i in range(total)]
        parts.append(lax.ppermute(block[None], "prow", pairs))
    return parts


def in_plane(parts, direction):
    stacked = jnp.concatenate(parts, 0)
    pieces = {0: stacked}
    if direction == 0:
        sent = {1: stacked, 2: stacked, 4: stacked}
    else:
        near, far = jnp.concatenate(parts[:2], 0), jnp.concatenate(parts[1:], 0)
        me = lax.axis_index("prow")
        sent = {}
        for bit in (1, 2, 4):
            after = (me & bit) != 0
            sent[bit] = jnp.where(after if direction > 0 else jnp.logical_not(after), far, near)
    for k in (2, 4, 6):
        pieces[k] = swap(sent[2 if k == 2 else 4], k)
    pieces[1] = swap(sent[1], 1)
    for k in (2, 4, 6):
        pieces[k + 1] = swap(pieces[k], 1)
    return [pieces[k] for k in range(PLANE)]


def gather(block, direction, pack):
    parts = along_z(block, direction)
    parts, packed = lax.optimization_barrier((parts, pack(block)))
    return in_plane(parts, direction), packed


def copy_window(side, pieces, xs, block, start, direction):
    me = lax.axis_index("prow")
    offset, parity = me & (PLANE - 1), (me & 1) ^ side
    size, lines = xs.shape[0], PLANE // 2
    pair = first_pair(start, parity)
    for k, piece in zip(range(side, PLANE, 2), pieces, strict=True):
        other = offset ^ k
        first = (other // 2 - pair) & (lines - 1)
        skipped = jnp.int32(0)
        if k > 0:
            skipped = (other > offset if direction > 0 else other < offset).astype(jnp.int32)
        for half in range(2):
            slot = first + half * lines
            source = 2 * (pair + slot) + parity
            apart = direction * (block // PLANE - source // PLANE)
            apart = jnp.clip(apart - skipped, 0, piece.shape[0] - 1)
            level = source // (PLANE * PLANES) if piece.shape[1] > 1 else 0
            at = pl.multiple_of(slot * size, size)
            xs[:, pl.ds(at, size)] = piece[apart, level]


def dot(left, right):
    return jnp.dot(left, right, preferred_element_type=jnp.float32)


def window_part(side, direction, row, rows, pieces, factor, xs):
    me = lax.axis_index("prow")
    size, half = xs.shape[0], SPAN // 2
    block = row * PLANE * PLANES + me
    start = window_start(block, direction, rows * PLANE * PLANES)
    copy_window(side, pieces, xs, block, start, direction)
    at = row * SPAN + side * half
    return dot(xs[...], factor[at : at + half].reshape(half * size, size))


def window_own_kernel(direction, *refs):
    pieces, (factor, part, xs) = refs[:4], refs[4:]
    for row in range(part.shape[0]):
        part[row] = window_part(0, direction, row, part.shape[0], pieces, factor, xs)


def window_other_kernel(direction, *refs):
    pieces, (factor, part, solved, known, xs) = refs[:4], refs[4:]
    for row in range(part.shape[0]):
        other = window_part(1, direction, row, part.shape[0], pieces, factor, xs)
        result = part[row] + other
        solved[row] = result
        known[row] = result.astype(known.dtype)


def backward_lower_kernel(*refs):
    pieces, (factor, part, upper, out, xs) = refs[:4], refs[4:]
    out[2, 0] = upper[0].T
    for row in range(2):
        out[row, 0] = (part[row] + window_part(1, -1, row, 2, pieces, factor, xs)).T


def down_kernel(odd, known, own, brought, near, level, far, table, out, xs):
    me = lax.axis_index("prow")
    plane = me // PLANE
    size = xs.shape[0]
    sources = ((own, 0, brought, 0), (near, 0, near, 4), (level, 0, level, 4), (far, 0, far, 4))
    for m in range(4):
        for slot in range(4):
            block = table[4 * (2 * m + odd) + slot]
            along = (block // PLANE) % PLANES ^ plane
            xs[:, slot * size : (slot + 1) * size] = known[along, block // (PLANE * PLANES)]
        factor, at = sources[m][2 * odd : 2 * odd + 2]
        out[m] = dot(xs[...], factor[at : at + 4].reshape(4 * size, size))


def correction_part(side, row, pieces, factor, xs):
    me = lax.axis_index("prow")
    offset, plane = me & (PLANE - 1), me // PLANE
    size = xs.shape[0]
    many = xs.shape[1] // size
    if row == 0:
        for k, piece in zip(range(side, PLANE, 2), pieces, strict=True):
            for along in range(PLANES):
                pair = (plane ^ along) * (PLANE // 2) + (offset ^ k) // 2
                xs[:, pl.ds(pl.multiple_of(pair * size, size), size)] = piece[along, 0]
    at = (2 * row + side) * many
    return dot(xs[...], factor[at : at + many].reshape(many * size, size))


def correction_own_kernel(*refs):
    pieces, (factor, part, xs) = refs[:4], refs[4:]
    for row in range(2):
        part[row] = correction_part(0, row, pieces, factor, xs)


def correction_kernel(*refs):
    pieces, (factor, part, solved, out, xs) = refs[:4], refs[4:]
    for row in range(2):
        result = part[row] + correction_part(1, row, pieces, factor, xs)
        known = solved[row].astype(out.dtype).astype(jnp.float32)
        rounded = result.astype(out.dtype).astype(jnp.float32)
        out[row] = (known - rounded).astype(out.dtype)


def turn_kernel(value, out):
    for row in range(3):
        out[row] = value[row, 0].astype(jnp.float32).T.astype(out.dtype)


def forward_out_kernel(lower, upper, out):
    for row in range(2):
        out[row, 0] = lower[row].T
    out[2, 0] = upper[0].T


def local_call(kernel, name, shapes, operands, width=0, tables=0):
    size = 128
    scratch = [pltpu.VMEM((size, width), jnp.bfloat16)] if width else []
    outs = [jax.ShapeDtypeStruct(*shape) for shape in shapes]
    return pl.pallas_call(
        kernel,
        out_shape=outs,
        in_specs=[pl.BlockSpec(memory_space=pltpu.VMEM)] * (len(operands) - tables)
        + [pl.BlockSpec(memory_space=pltpu.SMEM)] * tables,
        out_specs=[pl.BlockSpec(memory_space=pltpu.VMEM)] * len(outs),
        scratch_shapes=scratch,
        compiler_params=pltpu.CompilerParams(vmem_limit_bytes=VMEM_BYTES),
        cost_estimate=pl.CostEstimate(flops=0, bytes_accessed=1 << 20, transcendentals=0),
        name=name,
    )(*operands)


def fast_device(rhs, lower_factor_t, upper_factor_t, lower_snode, upper_snode, parent, pattern):
    rows, _, size, width = rhs.shape
    total = PLANE * PLANES
    f32, bf16 = jnp.float32, jnp.bfloat16

    def blocks(factor):
        return jnp.transpose(factor, (0, 1, 3, 4, 2, 5)).reshape(
            rows * total // 2, 2, rows, size, size
        )

    lower, upper = blocks(lower_factor_t), blocks(upper_factor_t)

    def line(values):
        return jnp.pad(values, ((0, 0), (0, 128 - values.shape[1])))

    rules = jnp.concatenate(
        [line(lower_snode[None]), line(upper_snode[None]), line(parent.T), line(pattern.T)], 0
    )
    own = local_call(turn_kernel, "turn", [((rows, width, size), bf16)], [rhs])[0]

    forward, backward, whole = 1, -1, 0
    half = SPAN // 2

    def level(factor, direction, count):
        first, base = (0, 0) if count == 2 else (2, 2 * total)
        kernel = functools.partial(pack_level_kernel, direction, base, count, first, count * total)
        return lambda after: pack_call(
            kernel, "pack_level", count * SPAN, 2 * count, factor, after, rules
        )

    def pack_up(after):
        return pack_call(pack_up_kernel, "pack_up", 2 * total, 4, upper, after, rules)

    def window(name, count, direction, pieces, packed):
        (part,) = local_call(
            functools.partial(window_own_kernel, direction),
            name + "_own",
            [((count, width, size), f32)],
            [*pieces[0::2], packed],
            half * size,
        )
        return local_call(
            functools.partial(window_other_kernel, direction),
            name,
            [((count, width, size), f32), ((count, width, size), bf16)],
            [*pieces[1::2], packed, part],
            half * size,
        )

    barrier = lax.optimization_barrier
    rhs_lower = own[:2]
    parts = along_z(rhs_lower, forward)
    packed = first_pack(lower, rhs_lower, rules)
    parts, (l1, even, odd, table) = barrier((parts, packed))
    pieces = in_plane(parts, forward)
    brought = swap(odd, 1)
    even, pieces[6] = barrier((even, pieces[6]))
    pairs = [
        jnp.concatenate([even[4 * m : 4 * m + 4], brought[4 * m : 4 * m + 4]], 0) for m in (1, 2, 3)
    ]
    down = [swap(pair, 2 * (m + 1)) for m, pair in enumerate(pairs)]
    solved, known = window("forward_lower", 2, forward, pieces, l1)
    parts = along_z(known, whole)
    parts[1], down = barrier((parts[1], down))
    held = jnp.concatenate(parts, 0)
    sums = []
    for group in (1, 0):
        sums += local_call(
            functools.partial(down_kernel, group),
            "coupling_other" if group else "coupling",
            [((4, width, size), f32)],
            [held, even, brought, *down, table],
            4 * size,
            1,
        )
    sums = sums[1] + swap(sums[0], 1)
    arrived = [swap(sums[m], 2 * m) for m in (1, 2, 3)]
    coupling = (sums[0] + arrived[0] + arrived[1] + arrived[2]).astype(bf16).astype(f32)
    difference = (own[2:].astype(f32) - coupling).astype(bf16)
    pieces, packed = gather(difference, forward, level(lower, forward, 1))
    forward_upper, upper_known = window("forward_upper", 1, forward, pieces, packed)
    pieces, packed = gather(upper_known, backward, level(upper, backward, 1))
    (forward_solution,) = local_call(
        forward_out_kernel,
        "forward_out",
        [((rows, 1, size, width), f32)],
        [solved, forward_upper],
    )
    backward_upper, back_known = window("backward_upper", 1, backward, pieces, packed)
    pieces, packed = gather(back_known, whole, pack_up)
    (part,) = local_call(
        correction_own_kernel,
        "correction_own",
        [((2, width, size), f32)],
        [*pieces[0::2], packed],
        total // 2 * size,
    )
    (remainder,) = local_call(
        correction_kernel,
        "correction",
        [((2, width, size), bf16)],
        [*pieces[1::2], packed, part, solved],
        total // 2 * size,
    )
    pieces, packed = gather(remainder, backward, level(upper, backward, 2))
    (part,) = local_call(
        functools.partial(window_own_kernel, backward),
        "backward_lower_own",
        [((2, width, size), f32)],
        [*pieces[0::2], packed],
        half * size,
    )
    (backward_solution,) = local_call(
        backward_lower_kernel,
        "backward_lower",
        [((rows, 1, size, width), f32)],
        [*pieces[1::2], packed, part, backward_upper],
        half * size,
    )
    return forward_solution, backward_solution


def block_masks(lower_snode, upper_snode, parent, pattern):
    count_lower = parent.shape[0]
    snode_ids = jnp.concatenate([lower_snode, upper_snode + count_lower])
    same = snode_ids[:, None] == snode_ids[None, :]
    onehot = (lower_snode[:, None] == jnp.arange(count_lower, dtype=jnp.int32)[None, :]).astype(
        jnp.int32
    )
    parent_block = jnp.sum(onehot * parent[:, 0][None, :], axis=1)
    pattern_block = jnp.sum(pattern[:, None, :] * onehot[None, :, :], axis=2)
    link = (upper_snode[:, None] == parent_block[None, :]) & (pattern_block == 1)
    return (same, link)


def couplings(link):
    upper_count, lower_count = link.shape
    total = upper_count + lower_count
    couple_lower = jnp.concatenate(
        [
            jnp.zeros((lower_count, total), bool),
            jnp.concatenate([link, jnp.zeros((upper_count, upper_count), bool)], 1),
        ],
        0,
    )
    couple_upper = jnp.concatenate(
        [
            jnp.concatenate([jnp.zeros((lower_count, lower_count), bool), link.T], 1),
            jnp.zeros((upper_count, total), bool),
        ],
        0,
    )
    return (couple_lower, couple_upper)


def on_device(rhs, lower_factor_t, upper_factor_t, lower_snode, upper_snode, parent, pattern):
    rows_axis = lax.axis_size("prow")
    row_index = lax.axis_index("prow")
    col_index = lax.axis_index("pcol")
    blocks_local = rhs.shape[0]
    sub_rows = rhs.shape[2]
    col_group = lower_factor_t.shape[1]
    block_size = lower_factor_t.shape[2]
    lower_local = lower_snode.shape[0] // rows_axis
    same, link = block_masks(lower_snode, upper_snode, parent, pattern)
    couple_lower, couple_upper = couplings(link)
    all_blocks = same.shape[0]

    def local_blocks(whole):
        selected = lax.dynamic_index_in_dim(
            whole.reshape(blocks_local, rows_axis, all_blocks), row_index, 1, keepdims=False
        )
        selected = selected.reshape(blocks_local, blocks_local, rows_axis)
        selected = lax.dynamic_slice_in_dim(selected, col_index * col_group, col_group, 2)
        return jnp.transpose(selected, (1, 2, 0)).reshape(
            blocks_local, col_group, 1, blocks_local, 1, 1
        )

    local_ids = jnp.arange(blocks_local, dtype=jnp.int32)
    row_elem = (
        (local_ids[:, None] * rows_axis + row_index) * block_size
        + jnp.arange(block_size, dtype=jnp.int32)[None, :]
    ).reshape(1, 1, 1, blocks_local, 1, block_size)
    own_cols = col_index * col_group + jnp.arange(col_group, dtype=jnp.int32)
    col_block = local_ids[:, None] * rows_axis + own_cols[None, :]
    col_elem = (
        col_block[:, :, None] * block_size + jnp.arange(block_size, dtype=jnp.int32)[None, None, :]
    ).reshape(blocks_local, col_group, block_size, 1, 1, 1)
    same_local = local_blocks(same)
    keep_lower = same_local & (row_elem >= col_elem) | local_blocks(couple_lower)
    keep_upper = same_local & (row_elem <= col_elem) | local_blocks(couple_upper)
    lower_kept = jnp.where(keep_lower, lower_factor_t, jnp.zeros((), lower_factor_t.dtype))
    upper_kept = jnp.where(keep_upper, upper_factor_t, jnp.zeros((), upper_factor_t.dtype))

    def apply_factor(factor, vector, col_range, row_range):
        window = factor[col_range[0] : col_range[1], :, :, row_range[0] : row_range[1], 0, :]
        pieces_in = lax.all_gather(vector, "prow", axis=1, tiled=True)
        selector = (
            jnp.arange(pieces_in.shape[1], dtype=jnp.int32)[:, None] == own_cols[None, :]
        ).astype(jnp.bfloat16)
        picked = jnp.einsum(
            "rjen,jq->rqen", pieces_in, selector, preferred_element_type=jnp.float32
        ).astype(jnp.bfloat16)
        summed = lax.dot_general(
            window, picked, (((0, 1, 2), (0, 1, 2)), ((), ())), preferred_element_type=jnp.float32
        )[:, None]
        return lax.psum(summed, "pcol")

    source = lax.all_gather(rhs, "pcol", axis=2, tiled=True)
    rhs_width = source.shape[3]
    lower_span = (0, lower_local)
    upper_span = (lower_local, blocks_local)
    rhs_lower = source[:lower_local]
    rhs_upper = source[lower_local:]
    forward_lower = apply_factor(lower_kept, rhs_lower, lower_span, lower_span)
    lower_known = forward_lower.astype(jnp.bfloat16)
    coupling = apply_factor(lower_kept, lower_known, lower_span, upper_span).astype(jnp.bfloat16)
    joined = apply_factor(
        lower_kept, jnp.concatenate([rhs_upper, coupling], 3), upper_span, upper_span
    )
    upper_direct = joined[..., :rhs_width]
    upper_update = joined[..., rhs_width:]
    forward_upper = upper_direct - upper_update
    upper_known = forward_upper.astype(jnp.bfloat16)
    backward_upper = apply_factor(upper_kept, upper_known, upper_span, upper_span)
    back_known = backward_upper.astype(jnp.bfloat16)
    correction = apply_factor(upper_kept, back_known, upper_span, lower_span).astype(jnp.bfloat16)
    joined_lower = apply_factor(
        upper_kept, jnp.concatenate([lower_known, correction], 3), lower_span, lower_span
    )
    lower_direct = joined_lower[..., :rhs_width]
    lower_update = joined_lower[..., rhs_width:]
    backward_lower = lower_direct - lower_update
    forward_solution = jnp.concatenate([forward_lower, forward_upper], 0)
    backward_solution = jnp.concatenate([backward_lower, backward_upper], 0)
    forward_solution = lax.dynamic_slice_in_dim(forward_solution, col_index * sub_rows, sub_rows, 2)
    backward_solution = lax.dynamic_slice_in_dim(
        backward_solution, col_index * sub_rows, sub_rows, 2
    )
    return (forward_solution, backward_solution)


def solution(mesh):
    placed = (
        P("parts", "prow", "pcol", None),
        P("parts", "pcol", None, None, "prow", None),
        P("parts", "pcol", None, None, "prow", None),
        P("parts"),
        P("parts"),
        P("parts", None),
        P("parts", None),
    )
    total = PLANE * PLANES
    simple = mesh.shape["prow"] == total and mesh.shape["pcol"] == 1
    return jax.shard_map(
        fast_device if simple else on_device,
        mesh=mesh,
        in_specs=placed,
        out_specs=(P("parts", "prow", "pcol", None), P("parts", "prow", "pcol", None)),
        check_vma=False,
    )
```

```python
import functools
import jax
import jax.numpy as jnp
from jax import lax
from jax.experimental import pallas as pl
from jax.experimental.pallas import tpu as pltpu
from jax.sharding import PartitionSpec as P

SPAN = 16
PLANE = 8
PLANES = 4
TURNS = ((4, 2, 6), (2, 4, 6))
VMEM_BYTES = 48 * 1024 * 1024


def window_start(block, direction, count):
    if direction > 0:
        return jnp.maximum(block - (SPAN - 1), 0)
    return jnp.minimum(block, count - SPAN)


def first_pair(start, parity):
    return (start + 1 - parity) // 2


def start_window(direction, base, rows, row_first, count, factor, out, sems):
    me = lax.axis_index("prow")
    half = SPAN // 2
    copies = []
    for row in range(rows):
        block = row * PLANE * PLANES + me
        start = window_start(block, direction, count)
        for side in range(2):
            parity = (me & 1) ^ side
            pair = first_pair(start, parity)
            at = row * SPAN + side * half
            copy = pltpu.make_async_copy(
                factor.at[pl.ds(base // 2 + pair, half), parity, row_first + row],
                out.at[pl.ds(at, half)],
                sems.at[2 * row + side],
            )
            copy.start()
            copies.append((copy, block, pair, side, at))
    return copies


def keep_window(direction, copies, snode, out):
    me = lax.axis_index("prow")
    half, size = SPAN // 2, out.shape[1]
    col = lax.broadcasted_iota(jnp.int32, (size, size), 0)
    line = lax.broadcasted_iota(jnp.int32, (size, size), 1)
    tri = line >= col if direction > 0 else line <= col
    zero = jnp.zeros((size, size), out.dtype)
    for copy, block, pair, side, at in copies:
        copy.wait()
        own = snode[block]
        for step in range(half):
            column = 2 * (pair + step) + ((me & 1) ^ side)
            kept = snode[column] == own
            kept = kept & (column <= block if direction > 0 else column >= block)
            out[at + step] = jnp.where(kept, out[at + step], zero)
        if side == 0:
            diagonal = at + block // 2 - pair
            out[diagonal] = jnp.where(tri, out[diagonal], zero)


def pack_level_kernel(direction, base, rows, row_first, count, factor, after, rules, out, sems):
    copies = start_window(direction, base, rows, row_first, count, factor, out, sems)
    keep_window(direction, copies, rules.at[0 if rows == 2 else 1], out)


def pack_up_kernel(factor, after, rules, out, sems):
    me = lax.axis_index("prow")
    total = PLANE * PLANES
    many, size = total // 2, out.shape[1]
    copies = []
    for row in range(2):
        for side in range(2):
            at = (2 * row + side) * many
            copy = pltpu.make_async_copy(
                factor.at[pl.ds(total, many), (me & 1) ^ side, row],
                out.at[pl.ds(at, many)],
                sems.at[2 * row + side],
            )
            copy.start()
            copies.append((copy, row, side, at))
    zero = jnp.zeros((size, size), out.dtype)
    for copy, row, side, at in copies:
        child = rules[0, row * total + me]
        above = rules[2, child]
        copy.wait()
        for pair in range(many):
            block = 2 * pair + ((me & 1) ^ side)
            linked = (above == rules[1, block]) & (rules[3 + child, block] == 1)
            out[at + pair] = jnp.where(linked, out[at + pair], zero)


def pack_call(kernel, name, blocks, copies, factor, after, rules):
    size, dtype = factor.shape[-1], factor.dtype
    return pl.pallas_call(
        kernel,
        out_shape=jax.ShapeDtypeStruct((blocks, size, size), dtype),
        in_specs=[pl.BlockSpec(memory_space=pl.ANY)] * 2
        + [pl.BlockSpec(memory_space=pltpu.SMEM)],
        out_specs=pl.BlockSpec(memory_space=pltpu.VMEM),
        scratch_shapes=[pltpu.SemaphoreType.DMA((copies,))],
        compiler_params=pltpu.CompilerParams(vmem_limit_bytes=VMEM_BYTES),
        cost_estimate=pl.CostEstimate(
            flops=0, bytes_accessed=2 * blocks * size * size * dtype.itemsize, transcendentals=0
        ),
        name=name,
    )(factor, after, rules)


def first_pack_kernel(
    factor, after, rules, mine, even, odd, table, kids, sems
):
    me = lax.axis_index("prow")
    offset, plane = me & (PLANE - 1), me // PLANE
    total = PLANE * PLANES
    count, children = 2 * total, rules.shape[0] - 3
    lower_snode, upper_snode, parent = rules.at[0], rules.at[1], rules.at[2]
    size = mine.shape[1]
    windows = start_window(1, 0, 2, 0, count, factor, mine, sems)
    begins = []
    for child in range(children):
        found = jnp.int32(0)
        for bit in reversed(range(count.bit_length() - 1)):
            ahead = found + (1 << bit)
            found = jnp.where(lower_snode[ahead - 1] < child, ahead, found)
        begins.append(found)
    parents = [parent[child] for child in range(children)]

    def children_of(above):
        first, first_at = jnp.int32(0), jnp.int32(0)
        last, last_at = jnp.int32(0), jnp.int32(0)
        for child in range(children):
            match = parents[child] == above
            last, last_at = jnp.where(match, child, last), jnp.where(match, begins[child], last_at)
        for child in reversed(range(children)):
            match = parents[child] == above
            first, first_at = jnp.where(match, child, first), jnp.where(match, begins[child], first_at)
        return (first, first_at), (last, last_at)

    def column(start, place, step):
        return start + ((place - start) & (PLANE - 1)) + step * PLANE

    low, high = children_of(upper_snode[me])
    copies = []
    for side, (child, start) in enumerate((low, high)):
        at = jnp.minimum(start, count - SPAN - 2)
        copy = pltpu.make_async_copy(
            factor.at[pl.ds(at // 2, SPAN // 2 + 1), :, 2], kids.at[side], sems.at[4 + side]
        )
        copy.start()
        linked = rules[3 + child, me] == 1
        if side:
            linked = linked & (low[0] != high[0])
        copies.append((copy, child, start, at, linked))
    for k in range(PLANE):
        pair = children_of(upper_snode[plane * PLANE + (offset ^ k)])
        for slot in range(4):
            found = column(pair[slot // 2][1], offset, slot % 2)
            table[4 * k + slot] = jnp.minimum(found, count - 1)
    keep_window(1, windows, lower_snode, mine)
    zero = jnp.zeros((size, size), mine.dtype)
    for side, (copy, child, start, at, linked) in enumerate(copies):
        copy.wait()
        for k in range(PLANE):
            for step in range(2):
                found = column(start, offset ^ k, step)
                source = jnp.minimum(found, count - 1)
                kept = linked & (found < count) & (lower_snode[source] == child)
                out = odd if k % 2 else even
                near = jnp.minimum(source // 2 - at // 2, SPAN // 2)
                value = kids[side, near, source % 2]
                out[4 * (k // 2) + 2 * side + step] = jnp.where(kept, value, zero)


def first_pack(factor, after, rules):
    size, dtype = factor.shape[-1], factor.dtype
    counts = (2 * SPAN, SPAN, SPAN)
    vmem, smem = (pl.BlockSpec(memory_space=space) for space in (pltpu.VMEM, pltpu.SMEM))
    return pl.pallas_call(
        first_pack_kernel,
        out_shape=[jax.ShapeDtypeStruct((count, size, size), dtype) for count in counts]
        + [jax.ShapeDtypeStruct((4 * PLANE,), jnp.int32)],
        in_specs=[pl.BlockSpec(memory_space=pl.ANY)] * 2 + [smem],
        out_specs=[vmem] * 3 + [smem],
        scratch_shapes=[
            pltpu.VMEM((2, SPAN // 2 + 1, 2, size, size), dtype),
            pltpu.SemaphoreType.DMA((6,)),
        ],
        compiler_params=pltpu.CompilerParams(vmem_limit_bytes=VMEM_BYTES),
        cost_estimate=pl.CostEstimate(
            flops=0, bytes_accessed=2 * sum(counts) * size * size * dtype.itemsize, transcendentals=0
        ),
        name="first_pack",
    )(factor, after, rules)


def swap(value, distance):
    return lax.ppermute(value, "prow", [(i, i ^ distance) for i in range(PLANE * PLANES)])


def along_z(block, direction):
    total = PLANE * PLANES
    parts = [block[None]]
    if direction == 0:
        return parts + [swap(block[None], PLANE * step) for step in range(1, PLANES)]
    for step in (1, 2):
        pairs = [(i, (i + direction * step * PLANE) % total) for i in range(total)]
        parts.append(lax.ppermute(block[None], "prow", pairs))
    return parts


def in_turn(value, distances):
    pairs = [(i, i ^ distances[i % 2]) for i in range(PLANE * PLANES)]
    return lax.ppermute(value, "prow", pairs)


def offsets_of(side):
    core = lax.axis_index("prow") & 1
    mine, other = TURNS if side == 0 else TURNS[::-1]
    return [side] + [jnp.where(core == 0, a, b) + side for a, b in zip(mine, other, strict=True)]


def in_plane(parts, direction):
    stacked = jnp.concatenate(parts, 0)
    me = lax.axis_index("prow")

    def sent(bit):
        if direction == 0:
            return stacked
        near, far = jnp.concatenate(parts[:2], 0), jnp.concatenate(parts[1:], 0)
        after = (me & bit) != 0
        return jnp.where(after if direction > 0 else jnp.logical_not(after), far, near)

    pieces = {0: stacked}
    for place, pair in enumerate(zip(*TURNS, strict=True)):
        bits = [2 if k == 2 else 4 for k in pair]
        pieces[2 * place + 2] = in_turn(sent(jnp.where((me & 1) == 0, *bits)), pair)
    pieces[1] = swap(sent(1), 1)
    for k in (2, 4, 6):
        pieces[k + 1] = swap(pieces[k], 1)
    return [pieces[k] for k in range(PLANE)]


def gather(block, direction, pack):
    parts = along_z(block, direction)
    parts, packed = lax.optimization_barrier((parts, pack(block)))
    return in_plane(parts, direction), packed


def copy_window(side, pieces, xs, block, start, direction):
    me = lax.axis_index("prow")
    offset, parity = me & (PLANE - 1), (me & 1) ^ side
    size, lines = xs.shape[0], PLANE // 2
    pair = first_pair(start, parity)
    for k, piece in zip(offsets_of(side), pieces, strict=True):
        other = offset ^ k
        first = (other // 2 - pair) & (lines - 1)
        skipped = (other > offset if direction > 0 else other < offset).astype(jnp.int32)
        for half in range(2):
            slot = first + half * lines
            source = 2 * (pair + slot) + parity
            apart = direction * (block // PLANE - source // PLANE)
            apart = jnp.clip(apart - skipped, 0, piece.shape[0] - 1)
            level = source // (PLANE * PLANES) if piece.shape[1] > 1 else 0
            at = pl.multiple_of(slot * size, size)
            xs[:, pl.ds(at, size)] = piece[apart, level]


def dot(left, right):
    return jnp.dot(left, right, preferred_element_type=jnp.float32)


def window_part(side, direction, row, rows, pieces, factor, xs):
    me = lax.axis_index("prow")
    size, half = xs.shape[0], SPAN // 2
    block = row * PLANE * PLANES + me
    start = window_start(block, direction, rows * PLANE * PLANES)
    copy_window(side, pieces, xs, block, start, direction)
    at = row * SPAN + side * half
    return dot(xs[...], factor[at : at + half].reshape(half * size, size))


def window_own_kernel(direction, *refs):
    pieces, (factor, part, xs) = refs[:4], refs[4:]
    for row in range(part.shape[0]):
        part[row] = window_part(0, direction, row, part.shape[0], pieces, factor, xs)


def window_other_kernel(direction, *refs):
    pieces, (factor, part, solved, known, xs) = refs[:4], refs[4:]
    for row in range(part.shape[0]):
        other = window_part(1, direction, row, part.shape[0], pieces, factor, xs)
        result = part[row] + other
        solved[row] = result
        known[row] = result.astype(known.dtype)


def backward_lower_kernel(*refs):
    pieces, (factor, part, upper, out, xs) = refs[:4], refs[4:]
    out[2, 0] = upper[0].T
    for row in range(2):
        out[row, 0] = (part[row] + window_part(1, -1, row, 2, pieces, factor, xs)).T


def down_kernel(odd, known, own, brought, near, level, far, table, out, xs):
    me = lax.axis_index("prow")
    plane = me // PLANE
    size = xs.shape[0]
    sources = ((own, 0, brought, 0), (near, 0, near, 4), (level, 0, level, 4), (far, 0, far, 4))
    for m, k in enumerate(offsets_of(0)):
        for slot in range(4):
            block = table[4 * (k + odd) + slot]
            along = (block // PLANE) % PLANES ^ plane
            xs[:, slot * size : (slot + 1) * size] = known[along, block // (PLANE * PLANES)]
        factor, at = sources[m][2 * odd : 2 * odd + 2]
        out[m] = dot(xs[...], factor[at : at + 4].reshape(4 * size, size))


def correction_part(side, row, pieces, factor, xs):
    me = lax.axis_index("prow")
    offset, plane = me & (PLANE - 1), me // PLANE
    size = xs.shape[0]
    many = xs.shape[1] // size
    if row == 0:
        for k, piece in zip(offsets_of(side), pieces, strict=True):
            for along in range(PLANES):
                pair = (plane ^ along) * (PLANE // 2) + (offset ^ k) // 2
                xs[:, pl.ds(pl.multiple_of(pair * size, size), size)] = piece[along, 0]
    at = (2 * row + side) * many
    return dot(xs[...], factor[at : at + many].reshape(many * size, size))


def correction_own_kernel(*refs):
    pieces, (factor, part, xs) = refs[:4], refs[4:]
    for row in range(2):
        part[row] = correction_part(0, row, pieces, factor, xs)


def correction_kernel(*refs):
    pieces, (factor, part, solved, out, xs) = refs[:4], refs[4:]
    for row in range(2):
        result = part[row] + correction_part(1, row, pieces, factor, xs)
        known = solved[row].astype(out.dtype).astype(jnp.float32)
        rounded = result.astype(out.dtype).astype(jnp.float32)
        out[row] = (known - rounded).astype(out.dtype)


def turn_kernel(value, out):
    for row in range(3):
        out[row] = value[row, 0].astype(jnp.float32).T.astype(out.dtype)


def forward_out_kernel(lower, upper, out):
    for row in range(2):
        out[row, 0] = lower[row].T
    out[2, 0] = upper[0].T


def local_call(kernel, name, shapes, operands, width=0, tables=0):
    size = 128
    scratch = [pltpu.VMEM((size, width), jnp.bfloat16)] if width else []
    outs = [jax.ShapeDtypeStruct(*shape) for shape in shapes]
    return pl.pallas_call(
        kernel,
        out_shape=outs,
        in_specs=[pl.BlockSpec(memory_space=pltpu.VMEM)] * (len(operands) - tables)
        + [pl.BlockSpec(memory_space=pltpu.SMEM)] * tables,
        out_specs=[pl.BlockSpec(memory_space=pltpu.VMEM)] * len(outs),
        scratch_shapes=scratch,
        compiler_params=pltpu.CompilerParams(vmem_limit_bytes=VMEM_BYTES),
        cost_estimate=pl.CostEstimate(flops=0, bytes_accessed=1 << 20, transcendentals=0),
        name=name,
    )(*operands)


def fast_device(rhs, lower_factor_t, upper_factor_t, lower_snode, upper_snode, parent, pattern):
    rows, _, size, width = rhs.shape
    total = PLANE * PLANES
    f32, bf16 = jnp.float32, jnp.bfloat16

    def blocks(factor):
        return jnp.transpose(factor, (0, 1, 3, 4, 2, 5)).reshape(
            rows * total // 2, 2, rows, size, size
        )

    lower, upper = blocks(lower_factor_t), blocks(upper_factor_t)

    def line(values):
        return jnp.pad(values, ((0, 0), (0, 128 - values.shape[1])))

    rules = jnp.concatenate(
        [line(lower_snode[None]), line(upper_snode[None]), line(parent.T), line(pattern.T)], 0
    )
    own = local_call(turn_kernel, "turn", [((rows, width, size), bf16)], [rhs])[0]

    forward, backward, whole = 1, -1, 0
    half = SPAN // 2

    def level(factor, direction, count):
        first, base = (0, 0) if count == 2 else (2, 2 * total)
        kernel = functools.partial(pack_level_kernel, direction, base, count, first, count * total)
        return lambda after: pack_call(
            kernel, "pack_level", count * SPAN, 2 * count, factor, after, rules
        )

    def pack_up(after):
        return pack_call(pack_up_kernel, "pack_up", 2 * total, 4, upper, after, rules)

    def window(name, count, direction, pieces, packed):
        (part,) = local_call(
            functools.partial(window_own_kernel, direction),
            name + "_own",
            [((count, width, size), f32)],
            [*pieces[0::2], packed],
            half * size,
        )
        return local_call(
            functools.partial(window_other_kernel, direction),
            name,
            [((count, width, size), f32), ((count, width, size), bf16)],
            [*pieces[1::2], packed, part],
            half * size,
        )

    barrier = lax.optimization_barrier
    rhs_lower = own[:2]
    parts = along_z(rhs_lower, forward)
    packed = first_pack(lower, rhs_lower, rules)
    l1, even, odd, table = packed
    parts, l1, even, table = barrier((parts, l1, even, table))
    pieces = in_plane(parts, forward)
    brought = swap(odd, 1)
    even, pieces[6] = barrier((even, pieces[6]))
    pairs = [
        jnp.concatenate([even[4 * m : 4 * m + 4], brought[4 * m : 4 * m + 4]], 0) for m in (1, 2, 3)
    ]
    turned = (lax.axis_index("prow") & 1) != 0
    down = [
        in_turn(jnp.where(turned, pairs[b // 2 - 1], pairs[a // 2 - 1]), (a, b))
        for a, b in zip(*TURNS, strict=True)
    ]
    solved, known = window("forward_lower", 2, forward, pieces, l1)
    parts = along_z(known, whole)
    parts[1], down = barrier((parts[1], down))
    held = jnp.concatenate(parts, 0)
    sums = []
    for group in (1, 0):
        sums += local_call(
            functools.partial(down_kernel, group),
            "coupling_other" if group else "coupling",
            [((4, width, size), f32)],
            [held, even, brought, *down, table],
            4 * size,
            1,
        )
    other = swap(sums[0], 1)
    places = [0] + [TURNS[1].index(k) + 1 for k in TURNS[0]]
    sums = [sums[1][m] + other[place] for m, place in enumerate(places)]
    arrived = [in_turn(sums[m + 1], pair) for m, pair in enumerate(zip(*TURNS, strict=True))]
    coupling = (sums[0] + arrived[0] + arrived[1] + arrived[2]).astype(bf16).astype(f32)
    difference = (own[2:].astype(f32) - coupling).astype(bf16)
    pieces, packed = gather(difference, forward, level(lower, forward, 1))
    forward_upper, upper_known = window("forward_upper", 1, forward, pieces, packed)
    upper_known, solved_now, upper_now = barrier((upper_known, solved, forward_upper))
    parts = along_z(upper_known, backward)
    (forward_solution,) = local_call(
        forward_out_kernel,
        "forward_out",
        [((rows, 1, size, width), f32)],
        [solved_now, upper_now],
    )
    packed = level(upper, backward, 1)(upper_known)
    parts, packed, forward_solution = barrier((parts, packed, forward_solution))
    pieces = in_plane(parts, backward)
    backward_upper, back_known = window("backward_upper", 1, backward, pieces, packed)
    pieces, packed = gather(back_known, whole, pack_up)
    (part,) = local_call(
        correction_own_kernel,
        "correction_own",
        [((2, width, size), f32)],
        [*pieces[0::2], packed],
        total // 2 * size,
    )
    (remainder,) = local_call(
        correction_kernel,
        "correction",
        [((2, width, size), bf16)],
        [*pieces[1::2], packed, part, solved],
        total // 2 * size,
    )
    pieces, packed = gather(remainder, backward, level(upper, backward, 2))
    (part,) = local_call(
        functools.partial(window_own_kernel, backward),
        "backward_lower_own",
        [((2, width, size), f32)],
        [*pieces[0::2], packed],
        half * size,
    )
    (backward_solution,) = local_call(
        backward_lower_kernel,
        "backward_lower",
        [((rows, 1, size, width), f32)],
        [*pieces[1::2], packed, part, backward_upper],
        half * size,
    )
    return forward_solution, backward_solution


def block_masks(lower_snode, upper_snode, parent, pattern):
    count_lower = parent.shape[0]
    snode_ids = jnp.concatenate([lower_snode, upper_snode + count_lower])
    same = snode_ids[:, None] == snode_ids[None, :]
    onehot = (lower_snode[:, None] == jnp.arange(count_lower, dtype=jnp.int32)[None, :]).astype(
        jnp.int32
    )
    parent_block = jnp.sum(onehot * parent[:, 0][None, :], axis=1)
    pattern_block = jnp.sum(pattern[:, None, :] * onehot[None, :, :], axis=2)
    link = (upper_snode[:, None] == parent_block[None, :]) & (pattern_block == 1)
    return (same, link)


def couplings(link):
    upper_count, lower_count = link.shape
    total = upper_count + lower_count
    couple_lower = jnp.concatenate(
        [
            jnp.zeros((lower_count, total), bool),
            jnp.concatenate([link, jnp.zeros((upper_count, upper_count), bool)], 1),
        ],
        0,
    )
    couple_upper = jnp.concatenate(
        [
            jnp.concatenate([jnp.zeros((lower_count, lower_count), bool), link.T], 1),
            jnp.zeros((upper_count, total), bool),
        ],
        0,
    )
    return (couple_lower, couple_upper)


def on_device(rhs, lower_factor_t, upper_factor_t, lower_snode, upper_snode, parent, pattern):
    rows_axis = lax.axis_size("prow")
    row_index = lax.axis_index("prow")
    col_index = lax.axis_index("pcol")
    blocks_local = rhs.shape[0]
    sub_rows = rhs.shape[2]
    col_group = lower_factor_t.shape[1]
    block_size = lower_factor_t.shape[2]
    lower_local = lower_snode.shape[0] // rows_axis
    same, link = block_masks(lower_snode, upper_snode, parent, pattern)
    couple_lower, couple_upper = couplings(link)
    all_blocks = same.shape[0]

    def local_blocks(whole):
        selected = lax.dynamic_index_in_dim(
            whole.reshape(blocks_local, rows_axis, all_blocks), row_index, 1, keepdims=False
        )
        selected = selected.reshape(blocks_local, blocks_local, rows_axis)
        selected = lax.dynamic_slice_in_dim(selected, col_index * col_group, col_group, 2)
        return jnp.transpose(selected, (1, 2, 0)).reshape(
            blocks_local, col_group, 1, blocks_local, 1, 1
        )

    local_ids = jnp.arange(blocks_local, dtype=jnp.int32)
    row_elem = (
        (local_ids[:, None] * rows_axis + row_index) * block_size
        + jnp.arange(block_size, dtype=jnp.int32)[None, :]
    ).reshape(1, 1, 1, blocks_local, 1, block_size)
    own_cols = col_index * col_group + jnp.arange(col_group, dtype=jnp.int32)
    col_block = local_ids[:, None] * rows_axis + own_cols[None, :]
    col_elem = (
        col_block[:, :, None] * block_size + jnp.arange(block_size, dtype=jnp.int32)[None, None, :]
    ).reshape(blocks_local, col_group, block_size, 1, 1, 1)
    same_local = local_blocks(same)
    keep_lower = same_local & (row_elem >= col_elem) | local_blocks(couple_lower)
    keep_upper = same_local & (row_elem <= col_elem) | local_blocks(couple_upper)
    lower_kept = jnp.where(keep_lower, lower_factor_t, jnp.zeros((), lower_factor_t.dtype))
    upper_kept = jnp.where(keep_upper, upper_factor_t, jnp.zeros((), upper_factor_t.dtype))

    def apply_factor(factor, vector, col_range, row_range):
        window = factor[col_range[0] : col_range[1], :, :, row_range[0] : row_range[1], 0, :]
        pieces_in = lax.all_gather(vector, "prow", axis=1, tiled=True)
        selector = (
            jnp.arange(pieces_in.shape[1], dtype=jnp.int32)[:, None] == own_cols[None, :]
        ).astype(jnp.bfloat16)
        picked = jnp.einsum(
            "rjen,jq->rqen", pieces_in, selector, preferred_element_type=jnp.float32
        ).astype(jnp.bfloat16)
        summed = lax.dot_general(
            window, picked, (((0, 1, 2), (0, 1, 2)), ((), ())), preferred_element_type=jnp.float32
        )[:, None]
        return lax.psum(summed, "pcol")

    source = lax.all_gather(rhs, "pcol", axis=2, tiled=True)
    rhs_width = source.shape[3]
    lower_span = (0, lower_local)
    upper_span = (lower_local, blocks_local)
    rhs_lower = source[:lower_local]
    rhs_upper = source[lower_local:]
    forward_lower = apply_factor(lower_kept, rhs_lower, lower_span, lower_span)
    lower_known = forward_lower.astype(jnp.bfloat16)
    coupling = apply_factor(lower_kept, lower_known, lower_span, upper_span).astype(jnp.bfloat16)
    joined = apply_factor(
        lower_kept, jnp.concatenate([rhs_upper, coupling], 3), upper_span, upper_span
    )
    upper_direct = joined[..., :rhs_width]
    upper_update = joined[..., rhs_width:]
    forward_upper = upper_direct - upper_update
    upper_known = forward_upper.astype(jnp.bfloat16)
    backward_upper = apply_factor(upper_kept, upper_known, upper_span, upper_span)
    back_known = backward_upper.astype(jnp.bfloat16)
    correction = apply_factor(upper_kept, back_known, upper_span, lower_span).astype(jnp.bfloat16)
    joined_lower = apply_factor(
        upper_kept, jnp.concatenate([lower_known, correction], 3), lower_span, lower_span
    )
    lower_direct = joined_lower[..., :rhs_width]
    lower_update = joined_lower[..., rhs_width:]
    backward_lower = lower_direct - lower_update
    forward_solution = jnp.concatenate([forward_lower, forward_upper], 0)
    backward_solution = jnp.concatenate([backward_lower, backward_upper], 0)
    forward_solution = lax.dynamic_slice_in_dim(forward_solution, col_index * sub_rows, sub_rows, 2)
    backward_solution = lax.dynamic_slice_in_dim(
        backward_solution, col_index * sub_rows, sub_rows, 2
    )
    return (forward_solution, backward_solution)


def solution(mesh):
    placed = (
        P("parts", "prow", "pcol", None),
        P("parts", "pcol", None, None, "prow", None),
        P("parts", "pcol", None, None, "prow", None),
        P("parts"),
        P("parts"),
        P("parts", None),
        P("parts", None),
    )
    total = PLANE * PLANES
    simple = mesh.shape["prow"] == total and mesh.shape["pcol"] == 1
    return jax.shard_map(
        fast_device if simple else on_device,
        mesh=mesh,
        in_specs=placed,
        out_specs=(P("parts", "prow", "pcol", None), P("parts", "prow", "pcol", None)),
        check_vma=False,
    )
```

```python
import functools
import jax
import jax.numpy as jnp
from jax import lax
from jax.experimental import pallas as pl
from jax.experimental.pallas import tpu as pltpu
from jax.sharding import PartitionSpec as P

SPAN = 16
PLANE = 8
PLANES = 4
TURNS = ((4, 2, 6), (2, 4, 6))
VMEM_BYTES = 48 * 1024 * 1024


def window_start(block, direction, count):
    if direction > 0:
        return jnp.maximum(block - (SPAN - 1), 0)
    return jnp.minimum(block, count - SPAN)


def first_pair(start, parity):
    return (start + 1 - parity) // 2


def start_window(direction, base, rows, row_first, count, factor, out, sems):
    me = lax.axis_index("prow")
    half = SPAN // 2
    copies = []
    for row in range(rows):
        block = row * PLANE * PLANES + me
        start = window_start(block, direction, count)
        for side in range(2):
            parity = (me & 1) ^ side
            pair = first_pair(start, parity)
            at = row * SPAN + side * half
            copy = pltpu.make_async_copy(
                factor.at[pl.ds(base // 2 + pair, half), parity, row_first + row],
                out.at[pl.ds(at, half)],
                sems.at[2 * row + side],
            )
            copy.start()
            copies.append((copy, block, pair, side, at))
    return copies


def keep_window(direction, copies, snode, out):
    me = lax.axis_index("prow")
    half, size = SPAN // 2, out.shape[1]
    col = lax.broadcasted_iota(jnp.int32, (size, size), 0)
    line = lax.broadcasted_iota(jnp.int32, (size, size), 1)
    tri = line >= col if direction > 0 else line <= col
    zero = jnp.zeros((size, size), out.dtype)
    for copy, block, pair, side, at in copies:
        copy.wait()
        own = snode[block]
        for step in range(half):
            column = 2 * (pair + step) + ((me & 1) ^ side)
            kept = snode[column] == own
            kept = kept & (column <= block if direction > 0 else column >= block)
            out[at + step] = jnp.where(kept, out[at + step], zero)
        if side == 0:
            diagonal = at + block // 2 - pair
            out[diagonal] = jnp.where(tri, out[diagonal], zero)


def pack_level_kernel(direction, base, rows, row_first, count, factor, after, rules, out, sems):
    copies = start_window(direction, base, rows, row_first, count, factor, out, sems)
    keep_window(direction, copies, rules.at[0 if rows == 2 else 1], out)


def pack_up_kernel(factor, after, rules, out, sems):
    me = lax.axis_index("prow")
    total = PLANE * PLANES
    many, size = total // 2, out.shape[1]
    copies = []
    for row in range(2):
        for side in range(2):
            at = (2 * row + side) * many
            copy = pltpu.make_async_copy(
                factor.at[pl.ds(total, many), (me & 1) ^ side, row],
                out.at[pl.ds(at, many)],
                sems.at[2 * row + side],
            )
            copy.start()
            copies.append((copy, row, side, at))
    zero = jnp.zeros((size, size), out.dtype)
    for copy, row, side, at in copies:
        child = rules[0, row * total + me]
        above = rules[2, child]
        copy.wait()
        for pair in range(many):
            block = 2 * pair + ((me & 1) ^ side)
            linked = (above == rules[1, block]) & (rules[3 + child, block] == 1)
            out[at + pair] = jnp.where(linked, out[at + pair], zero)


def pack_call(kernel, name, blocks, copies, factor, after, rules):
    size, dtype = factor.shape[-1], factor.dtype
    return pl.pallas_call(
        kernel,
        out_shape=jax.ShapeDtypeStruct((blocks, size, size), dtype),
        in_specs=[pl.BlockSpec(memory_space=pl.ANY)] * 2
        + [pl.BlockSpec(memory_space=pltpu.SMEM)],
        out_specs=pl.BlockSpec(memory_space=pltpu.VMEM),
        scratch_shapes=[pltpu.SemaphoreType.DMA((copies,))],
        compiler_params=pltpu.CompilerParams(vmem_limit_bytes=VMEM_BYTES),
        cost_estimate=pl.CostEstimate(
            flops=0, bytes_accessed=2 * blocks * size * size * dtype.itemsize, transcendentals=0
        ),
        name=name,
    )(factor, after, rules)


def first_pack_kernel(
    factor, after, rules, mine, even, odd, table, kids, sems
):
    me = lax.axis_index("prow")
    offset, plane = me & (PLANE - 1), me // PLANE
    total = PLANE * PLANES
    count, children = 2 * total, rules.shape[0] - 3
    lower_snode, upper_snode, parent = rules.at[0], rules.at[1], rules.at[2]
    size = mine.shape[1]
    windows = start_window(1, 0, 2, 0, count, factor, mine, sems)
    begins = []
    for child in range(children):
        found = jnp.int32(0)
        for bit in reversed(range(count.bit_length() - 1)):
            ahead = found + (1 << bit)
            found = jnp.where(lower_snode[ahead - 1] < child, ahead, found)
        begins.append(found)
    parents = [parent[child] for child in range(children)]

    def children_of(above):
        first, first_at = jnp.int32(0), jnp.int32(0)
        last, last_at = jnp.int32(0), jnp.int32(0)
        for child in range(children):
            match = parents[child] == above
            last, last_at = jnp.where(match, child, last), jnp.where(match, begins[child], last_at)
        for child in reversed(range(children)):
            match = parents[child] == above
            first, first_at = jnp.where(match, child, first), jnp.where(match, begins[child], first_at)
        return (first, first_at), (last, last_at)

    def column(start, place, step):
        return start + ((place - start) & (PLANE - 1)) + step * PLANE

    low, high = children_of(upper_snode[me])
    copies = []
    for side, (child, start) in enumerate((low, high)):
        at = jnp.minimum(start, count - SPAN - 2)
        copy = pltpu.make_async_copy(
            factor.at[pl.ds(at // 2, SPAN // 2 + 1), :, 2], kids.at[side], sems.at[4 + side]
        )
        copy.start()
        linked = rules[3 + child, me] == 1
        if side:
            linked = linked & (low[0] != high[0])
        copies.append((copy, child, start, at, linked))
    for k in range(PLANE):
        pair = children_of(upper_snode[plane * PLANE + (offset ^ k)])
        for slot in range(4):
            found = column(pair[slot // 2][1], offset, slot % 2)
            table[4 * k + slot] = jnp.minimum(found, count - 1)
    keep_window(1, windows, lower_snode, mine)
    zero = jnp.zeros((size, size), mine.dtype)
    for side, (copy, child, start, at, linked) in enumerate(copies):
        copy.wait()
        for k in range(PLANE):
            for step in range(2):
                found = column(start, offset ^ k, step)
                source = jnp.minimum(found, count - 1)
                kept = linked & (found < count) & (lower_snode[source] == child)
                out = odd if k % 2 else even
                near = jnp.minimum(source // 2 - at // 2, SPAN // 2)
                value = kids[side, near, source % 2]
                out[4 * (k // 2) + 2 * side + step] = jnp.where(kept, value, zero)


def first_pack(factor, after, rules):
    size, dtype = factor.shape[-1], factor.dtype
    counts = (2 * SPAN, SPAN, SPAN)
    vmem, smem = (pl.BlockSpec(memory_space=space) for space in (pltpu.VMEM, pltpu.SMEM))
    return pl.pallas_call(
        first_pack_kernel,
        out_shape=[jax.ShapeDtypeStruct((count, size, size), dtype) for count in counts]
        + [jax.ShapeDtypeStruct((4 * PLANE,), jnp.int32)],
        in_specs=[pl.BlockSpec(memory_space=pl.ANY)] * 2 + [smem],
        out_specs=[vmem] * 3 + [smem],
        scratch_shapes=[
            pltpu.VMEM((2, SPAN // 2 + 1, 2, size, size), dtype),
            pltpu.SemaphoreType.DMA((6,)),
        ],
        compiler_params=pltpu.CompilerParams(vmem_limit_bytes=VMEM_BYTES),
        cost_estimate=pl.CostEstimate(
            flops=0, bytes_accessed=2 * sum(counts) * size * size * dtype.itemsize, transcendentals=0
        ),
        name="first_pack",
    )(factor, after, rules)


def swap(value, distance):
    return lax.ppermute(value, "prow", [(i, i ^ distance) for i in range(PLANE * PLANES)])


def along_z(block, direction):
    total = PLANE * PLANES
    parts = [block[None]]
    if direction == 0:
        return parts + [swap(block[None], PLANE * step) for step in range(1, PLANES)]
    for step in (1, 2):
        pairs = [(i, (i + direction * step * PLANE) % total) for i in range(total)]
        parts.append(lax.ppermute(block[None], "prow", pairs))
    return parts


def in_turn(value, distances):
    pairs = [(i, i ^ distances[i % 2]) for i in range(PLANE * PLANES)]
    return lax.ppermute(value, "prow", pairs)


def offsets_of(side):
    core = lax.axis_index("prow") & 1
    mine, other = TURNS if side == 0 else TURNS[::-1]
    return [side] + [jnp.where(core == 0, a, b) + side for a, b in zip(mine, other, strict=True)]


def in_plane(parts, direction):
    stacked = jnp.concatenate(parts, 0)
    me = lax.axis_index("prow")

    def sent(bit):
        if direction == 0:
            return stacked
        near, far = jnp.concatenate(parts[:2], 0), jnp.concatenate(parts[1:], 0)
        after = (me & bit) != 0
        return jnp.where(after if direction > 0 else jnp.logical_not(after), far, near)

    pieces = {0: stacked}
    for place, pair in enumerate(zip(*TURNS, strict=True)):
        bits = [2 if k == 2 else 4 for k in pair]
        pieces[2 * place + 2] = in_turn(sent(jnp.where((me & 1) == 0, *bits)), pair)
    pieces[1] = swap(sent(1), 1)
    for k in (2, 4, 6):
        pieces[k + 1] = swap(pieces[k], 1)
    return [pieces[k] for k in range(PLANE)]


def gather(block, direction, pack):
    parts = along_z(block, direction)
    parts, packed = lax.optimization_barrier((parts, pack(block)))
    return in_plane(parts, direction), packed


def copy_window(side, pieces, xs, block, start, direction, stream):
    me = lax.axis_index("prow")
    offset, parity = me & (PLANE - 1), (me & 1) ^ side
    size, lines = xs.shape[0], PLANE // 2
    pair = first_pair(start, parity)
    for k, piece in zip(offsets_of(side), pieces, strict=True):
        other = offset ^ k
        first = (other // 2 - pair) & (lines - 1)
        skipped = (other > offset if direction > 0 else other < offset).astype(jnp.int32)
        for half in range(2):
            slot = first + half * lines
            source = 2 * (pair + slot) + parity
            apart = direction * (block // PLANE - source // PLANE)
            apart = jnp.clip(apart - skipped, 0, piece.shape[0] - 1)
            level = source // (PLANE * PLANES) if stream is None else stream
            at = pl.multiple_of(slot * size, size)
            xs[:, pl.ds(at, size)] = piece[apart, level]


def dot(left, right):
    return jnp.dot(left, right, preferred_element_type=jnp.float32)


def window_part(side, direction, row, rows, pieces, factor, xs):
    me = lax.axis_index("prow")
    size, half = xs.shape[0], SPAN // 2
    block = row * PLANE * PLANES + me
    start = window_start(block, direction, rows * PLANE * PLANES)
    at = row * SPAN + side * half
    result = None
    for stream in range(pieces[0].shape[1]) if rows == 1 else (None,):
        copy_window(side, pieces, xs, block, start, direction, stream)
        term = dot(xs[...], factor[at : at + half].reshape(half * size, size))
        result = term if result is None else result + term
    return result


def window_own_kernel(direction, *refs):
    pieces, (factor, part, xs) = refs[:4], refs[4:]
    for row in range(part.shape[0]):
        part[row] = window_part(0, direction, row, part.shape[0], pieces, factor, xs)


def window_other_kernel(direction, *refs):
    pieces, (factor, part, solved, known, xs) = refs[:4], refs[4:]
    for row in range(part.shape[0]):
        other = window_part(1, direction, row, part.shape[0], pieces, factor, xs)
        result = part[row] + other
        solved[row] = result
        known[row] = result.astype(known.dtype)


def backward_lower_kernel(*refs):
    pieces, (factor, part, upper, out, xs) = refs[:4], refs[4:]
    out[2, 0] = upper[0].T
    for row in range(2):
        out[row, 0] = (part[row] + window_part(1, -1, row, 2, pieces, factor, xs)).T


def down_kernel(odd, known, own, brought, near, level, far, table, out, xs):
    me = lax.axis_index("prow")
    plane = me // PLANE
    size = xs.shape[0]
    sources = ((own, 0, brought, 0), (near, 0, near, 4), (level, 0, level, 4), (far, 0, far, 4))
    for m, k in enumerate(offsets_of(0)):
        for slot in range(4):
            block = table[4 * (k + odd) + slot]
            along = (block // PLANE) % PLANES ^ plane
            xs[:, slot * size : (slot + 1) * size] = known[along, block // (PLANE * PLANES)]
        factor, at = sources[m][2 * odd : 2 * odd + 2]
        out[m] = dot(xs[...], factor[at : at + 4].reshape(4 * size, size))


def correction_part(side, row, pieces, factor, xs):
    me = lax.axis_index("prow")
    offset, plane = me & (PLANE - 1), me // PLANE
    size = xs.shape[0]
    many = xs.shape[1] // size
    if row == 0:
        for k, piece in zip(offsets_of(side), pieces, strict=True):
            for along in range(PLANES):
                pair = (plane ^ along) * (PLANE // 2) + (offset ^ k) // 2
                xs[:, pl.ds(pl.multiple_of(pair * size, size), size)] = piece[along, 0]
    at = (2 * row + side) * many
    return dot(xs[...], factor[at : at + many].reshape(many * size, size))


def correction_own_kernel(*refs):
    pieces, (factor, part, xs) = refs[:4], refs[4:]
    for row in range(2):
        part[row] = correction_part(0, row, pieces, factor, xs)


def correction_kernel(*refs):
    pieces, (factor, part, solved, out, xs) = refs[:4], refs[4:]
    for row in range(2):
        result = part[row] + correction_part(1, row, pieces, factor, xs)
        known = solved[row].astype(out.dtype).astype(jnp.float32)
        rounded = result.astype(out.dtype).astype(jnp.float32)
        out[row] = (known - rounded).astype(out.dtype)


def turn_kernel(value, out):
    for row in range(3):
        out[row] = value[row, 0].astype(jnp.float32).T.astype(out.dtype)


def forward_out_kernel(lower, upper, out):
    for row in range(2):
        out[row, 0] = lower[row].T
    out[2, 0] = upper[0].T


def local_call(kernel, name, shapes, operands, width=0, tables=0):
    size = 128
    scratch = [pltpu.VMEM((size, width), jnp.bfloat16)] if width else []
    outs = [jax.ShapeDtypeStruct(*shape) for shape in shapes]
    return pl.pallas_call(
        kernel,
        out_shape=outs,
        in_specs=[pl.BlockSpec(memory_space=pltpu.VMEM)] * (len(operands) - tables)
        + [pl.BlockSpec(memory_space=pltpu.SMEM)] * tables,
        out_specs=[pl.BlockSpec(memory_space=pltpu.VMEM)] * len(outs),
        scratch_shapes=scratch,
        compiler_params=pltpu.CompilerParams(vmem_limit_bytes=VMEM_BYTES),
        cost_estimate=pl.CostEstimate(flops=0, bytes_accessed=1 << 20, transcendentals=0),
        name=name,
    )(*operands)


def fast_device(rhs, lower_factor_t, upper_factor_t, lower_snode, upper_snode, parent, pattern):
    rows, _, size, width = rhs.shape
    total = PLANE * PLANES
    f32, bf16 = jnp.float32, jnp.bfloat16

    def blocks(factor):
        return jnp.transpose(factor, (0, 1, 3, 4, 2, 5)).reshape(
            rows * total // 2, 2, rows, size, size
        )

    lower, upper = blocks(lower_factor_t), blocks(upper_factor_t)

    def line(values):
        return jnp.pad(values, ((0, 0), (0, 128 - values.shape[1])))

    rules = jnp.concatenate(
        [line(lower_snode[None]), line(upper_snode[None]), line(parent.T), line(pattern.T)], 0
    )
    own = local_call(turn_kernel, "turn", [((rows, width, size), bf16)], [rhs])[0]

    forward, backward, whole = 1, -1, 0
    half = SPAN // 2

    def level(factor, direction, count):
        first, base = (0, 0) if count == 2 else (2, 2 * total)
        kernel = functools.partial(pack_level_kernel, direction, base, count, first, count * total)
        return lambda after: pack_call(
            kernel, "pack_level", count * SPAN, 2 * count, factor, after, rules
        )

    def pack_up(after):
        return pack_call(pack_up_kernel, "pack_up", 2 * total, 4, upper, after, rules)

    def window(name, count, direction, pieces, packed):
        (part,) = local_call(
            functools.partial(window_own_kernel, direction),
            name + "_own",
            [((count, width, size), f32)],
            [*pieces[0::2], packed],
            half * size,
        )
        return local_call(
            functools.partial(window_other_kernel, direction),
            name,
            [((count, width, size), f32), ((count, width, size), bf16)],
            [*pieces[1::2], packed, part],
            half * size,
        )

    barrier = lax.optimization_barrier
    rhs_lower = own[:2]
    parts = along_z(rhs_lower, forward)
    packed = first_pack(lower, rhs_lower, rules)
    l1, even, odd, table = packed
    parts, l1, even, table = barrier((parts, l1, even, table))
    pieces = in_plane(parts, forward)
    brought = swap(odd, 1)
    even, pieces[6] = barrier((even, pieces[6]))
    pairs = [
        jnp.concatenate([even[4 * m : 4 * m + 4], brought[4 * m : 4 * m + 4]], 0) for m in (1, 2, 3)
    ]
    turned = (lax.axis_index("prow") & 1) != 0
    down = [
        in_turn(jnp.where(turned, pairs[b // 2 - 1], pairs[a // 2 - 1]), (a, b))
        for a, b in zip(*TURNS, strict=True)
    ]
    solved, known = window("forward_lower", 2, forward, pieces, l1)
    parts = along_z(known, whole)
    parts[1], down = barrier((parts[1], down))
    held = jnp.concatenate(parts, 0)
    sums = []
    for group in (1, 0):
        sums += local_call(
            functools.partial(down_kernel, group),
            "coupling_other" if group else "coupling",
            [((4, width, size), f32)],
            [held, even, brought, *down, table],
            4 * size,
            1,
        )
    other = swap(sums[0], 1)
    places = [0] + [TURNS[1].index(k) + 1 for k in TURNS[0]]
    sums = [sums[1][m] + other[place] for m, place in enumerate(places)]
    arrived = [in_turn(sums[m + 1], pair) for m, pair in enumerate(zip(*TURNS, strict=True))]
    coupling = (sums[0] + arrived[0] + arrived[1] + arrived[2]).astype(bf16)
    streams = jnp.concatenate([own[2:], -coupling[None]], 0)
    pieces, packed = gather(streams, forward, level(lower, forward, 1))
    forward_upper, upper_known = window("forward_upper", 1, forward, pieces, packed)
    upper_known, solved_now, upper_now = barrier((upper_known, solved, forward_upper))
    parts = along_z(upper_known, backward)
    (forward_solution,) = local_call(
        forward_out_kernel,
        "forward_out",
        [((rows, 1, size, width), f32)],
        [solved_now, upper_now],
    )
    packed = level(upper, backward, 1)(upper_known)
    parts, packed, forward_solution = barrier((parts, packed, forward_solution))
    pieces = in_plane(parts, backward)
    backward_upper, back_known = window("backward_upper", 1, backward, pieces, packed)
    pieces, packed = gather(back_known, whole, pack_up)
    (part,) = local_call(
        correction_own_kernel,
        "correction_own",
        [((2, width, size), f32)],
        [*pieces[0::2], packed],
        total // 2 * size,
    )
    (remainder,) = local_call(
        correction_kernel,
        "correction",
        [((2, width, size), bf16)],
        [*pieces[1::2], packed, part, solved],
        total // 2 * size,
    )
    pieces, packed = gather(remainder, backward, level(upper, backward, 2))
    (part,) = local_call(
        functools.partial(window_own_kernel, backward),
        "backward_lower_own",
        [((2, width, size), f32)],
        [*pieces[0::2], packed],
        half * size,
    )
    (backward_solution,) = local_call(
        backward_lower_kernel,
        "backward_lower",
        [((rows, 1, size, width), f32)],
        [*pieces[1::2], packed, part, backward_upper],
        half * size,
    )
    return forward_solution, backward_solution


def block_masks(lower_snode, upper_snode, parent, pattern):
    count_lower = parent.shape[0]
    snode_ids = jnp.concatenate([lower_snode, upper_snode + count_lower])
    same = snode_ids[:, None] == snode_ids[None, :]
    onehot = (lower_snode[:, None] == jnp.arange(count_lower, dtype=jnp.int32)[None, :]).astype(
        jnp.int32
    )
    parent_block = jnp.sum(onehot * parent[:, 0][None, :], axis=1)
    pattern_block = jnp.sum(pattern[:, None, :] * onehot[None, :, :], axis=2)
    link = (upper_snode[:, None] == parent_block[None, :]) & (pattern_block == 1)
    return (same, link)


def couplings(link):
    upper_count, lower_count = link.shape
    total = upper_count + lower_count
    couple_lower = jnp.concatenate(
        [
            jnp.zeros((lower_count, total), bool),
            jnp.concatenate([link, jnp.zeros((upper_count, upper_count), bool)], 1),
        ],
        0,
    )
    couple_upper = jnp.concatenate(
        [
            jnp.concatenate([jnp.zeros((lower_count, lower_count), bool), link.T], 1),
            jnp.zeros((upper_count, total), bool),
        ],
        0,
    )
    return (couple_lower, couple_upper)


def on_device(rhs, lower_factor_t, upper_factor_t, lower_snode, upper_snode, parent, pattern):
    rows_axis = lax.axis_size("prow")
    row_index = lax.axis_index("prow")
    col_index = lax.axis_index("pcol")
    blocks_local = rhs.shape[0]
    sub_rows = rhs.shape[2]
    col_group = lower_factor_t.shape[1]
    block_size = lower_factor_t.shape[2]
    lower_local = lower_snode.shape[0] // rows_axis
    same, link = block_masks(lower_snode, upper_snode, parent, pattern)
    couple_lower, couple_upper = couplings(link)
    all_blocks = same.shape[0]

    def local_blocks(whole):
        selected = lax.dynamic_index_in_dim(
            whole.reshape(blocks_local, rows_axis, all_blocks), row_index, 1, keepdims=False
        )
        selected = selected.reshape(blocks_local, blocks_local, rows_axis)
        selected = lax.dynamic_slice_in_dim(selected, col_index * col_group, col_group, 2)
        return jnp.transpose(selected, (1, 2, 0)).reshape(
            blocks_local, col_group, 1, blocks_local, 1, 1
        )

    local_ids = jnp.arange(blocks_local, dtype=jnp.int32)
    row_elem = (
        (local_ids[:, None] * rows_axis + row_index) * block_size
        + jnp.arange(block_size, dtype=jnp.int32)[None, :]
    ).reshape(1, 1, 1, blocks_local, 1, block_size)
    own_cols = col_index * col_group + jnp.arange(col_group, dtype=jnp.int32)
    col_block = local_ids[:, None] * rows_axis + own_cols[None, :]
    col_elem = (
        col_block[:, :, None] * block_size + jnp.arange(block_size, dtype=jnp.int32)[None, None, :]
    ).reshape(blocks_local, col_group, block_size, 1, 1, 1)
    same_local = local_blocks(same)
    keep_lower = same_local & (row_elem >= col_elem) | local_blocks(couple_lower)
    keep_upper = same_local & (row_elem <= col_elem) | local_blocks(couple_upper)
    lower_kept = jnp.where(keep_lower, lower_factor_t, jnp.zeros((), lower_factor_t.dtype))
    upper_kept = jnp.where(keep_upper, upper_factor_t, jnp.zeros((), upper_factor_t.dtype))

    def apply_factor(factor, vector, col_range, row_range):
        window = factor[col_range[0] : col_range[1], :, :, row_range[0] : row_range[1], 0, :]
        pieces_in = lax.all_gather(vector, "prow", axis=1, tiled=True)
        selector = (
            jnp.arange(pieces_in.shape[1], dtype=jnp.int32)[:, None] == own_cols[None, :]
        ).astype(jnp.bfloat16)
        picked = jnp.einsum(
            "rjen,jq->rqen", pieces_in, selector, preferred_element_type=jnp.float32
        ).astype(jnp.bfloat16)
        summed = lax.dot_general(
            window, picked, (((0, 1, 2), (0, 1, 2)), ((), ())), preferred_element_type=jnp.float32
        )[:, None]
        return lax.psum(summed, "pcol")

    source = lax.all_gather(rhs, "pcol", axis=2, tiled=True)
    rhs_width = source.shape[3]
    lower_span = (0, lower_local)
    upper_span = (lower_local, blocks_local)
    rhs_lower = source[:lower_local]
    rhs_upper = source[lower_local:]
    forward_lower = apply_factor(lower_kept, rhs_lower, lower_span, lower_span)
    lower_known = forward_lower.astype(jnp.bfloat16)
    coupling = apply_factor(lower_kept, lower_known, lower_span, upper_span).astype(jnp.bfloat16)
    joined = apply_factor(
        lower_kept, jnp.concatenate([rhs_upper, coupling], 3), upper_span, upper_span
    )
    upper_direct = joined[..., :rhs_width]
    upper_update = joined[..., rhs_width:]
    forward_upper = upper_direct - upper_update
    upper_known = forward_upper.astype(jnp.bfloat16)
    backward_upper = apply_factor(upper_kept, upper_known, upper_span, upper_span)
    back_known = backward_upper.astype(jnp.bfloat16)
    correction = apply_factor(upper_kept, back_known, upper_span, lower_span).astype(jnp.bfloat16)
    joined_lower = apply_factor(
        upper_kept, jnp.concatenate([lower_known, correction], 3), lower_span, lower_span
    )
    lower_direct = joined_lower[..., :rhs_width]
    lower_update = joined_lower[..., rhs_width:]
    backward_lower = lower_direct - lower_update
    forward_solution = jnp.concatenate([forward_lower, forward_upper], 0)
    backward_solution = jnp.concatenate([backward_lower, backward_upper], 0)
    forward_solution = lax.dynamic_slice_in_dim(forward_solution, col_index * sub_rows, sub_rows, 2)
    backward_solution = lax.dynamic_slice_in_dim(
        backward_solution, col_index * sub_rows, sub_rows, 2
    )
    return (forward_solution, backward_solution)


def solution(mesh):
    placed = (
        P("parts", "prow", "pcol", None),
        P("parts", "pcol", None, None, "prow", None),
        P("parts", "pcol", None, None, "prow", None),
        P("parts"),
        P("parts"),
        P("parts", None),
        P("parts", None),
    )
    total = PLANE * PLANES
    simple = mesh.shape["prow"] == total and mesh.shape["pcol"] == 1
    return jax.shard_map(
        fast_device if simple else on_device,
        mesh=mesh,
        in_specs=placed,
        out_specs=(P("parts", "prow", "pcol", None), P("parts", "prow", "pcol", None)),
        check_vma=False,
    )
```
